256 devices in a mesh: lon: 16 (over x, y_hi, core), lat: 16 (over z, y_lo).
Axes of the slice: x: 4, y: 4 (y_hi: 2, y_lo: 2; y = y_hi * 2 + y_lo), z: 8, core: 2. Of those that a mesh axis runs over, the one named last changes fastest.
Arguments:
- zonal_current: float32 [4, 512, 16384], P(None, 'lat', 'lon'), may hold values from -6 to 6
- meridian_current: float32 [4, 512, 16384], P(None, 'lat', 'lon'), may hold values from -6 to 6
- thermal_deviation: float32 [4, 512, 16384], P(None, 'lat', 'lon'), may hold values from -6 to 6
- saltiness_deviation: float32 [4, 512, 16384], P(None, 'lat', 'lon'), may hold values from -6 to 6
- dye_quantity: float32 [4, 512, 16384], P(None, 'lat', 'lon'), may hold values from -6 to 6
- water_indicator: int32 [4, 512, 16384], P(None, 'lat', 'lon'), may hold values from 0 to 1, as said below
Outputs:
- zonal_out: float32 [4, 512, 16384], P(None, 'lat', 'lon')
- meridional_out: float32 [4, 512, 16384], P(None, 'lat', 'lon')
- temperature_out: float32 [4, 512, 16384], P(None, 'lat', 'lon')
- salinity_out: float32 [4, 512, 16384], P(None, 'lat', 'lon')
- tracer_out: float32 [4, 512, 16384], P(None, 'lat', 'lon')
The draws below stay inside these ranges and needn't reach their ends.
Inputs may be any that keep to these rules, and one draw needn't show every extreme that they name: `water_indicator`: A cell that is sea at some level is sea at every level above it.
All inputs are finite; a program needn't handle non-finite values.
Results may differ from the reference program's by a relative error of at most 0.00002.
Values sent between devices are 32-bit elements; how exact they have to be, the bound alone decides.
No kernel may reach another device: no remote copies, remote signals or barrier semaphores. Data moves between devices by JAX's collectives and lax.ppermute only.
A program may use at most 64 MiB of HBM per device.

```python
import jax
import jax.numpy as jnp

DEPTH_SHEETS = 4
STEPS = 2
MERIDIAN_TOTAL = 16384
PARALLEL_TOTAL = 512


def draw_water_indicator(key, part):
    key = jax.random.fold_in(key, 7)
    depth_levels = jax.random.randint(key, (PARALLEL_TOTAL, MERIDIAN_TOTAL), 0, DEPTH_SHEETS + 1)
    level_index = jnp.arange(DEPTH_SHEETS, dtype=jnp.int32)[:, None, None]
    return (level_index < depth_levels[None]).astype(jnp.int32)


def steps_of(key, extent, split, least, high):
    gain, own = 1.0, jax.random.fold_in(key, 6)
    for position, parts in split:
        steps = jnp.exp(jax.random.uniform(jax.random.fold_in(own, position), (parts,), jnp.float32, least / len(split), high / len(split)))
        gain = gain * jnp.repeat(steps, extent[position] // parts).reshape([-1 if axis == position else 1 for axis in range(len(extent))])
    return gain


def normal_values(rng, shape, width, most, cuts=(), kind=jnp.bfloat16):
    values = jax.random.normal(rng, shape, jnp.float32) * width
    if len(cuts) > 0:
        values = steps_of(rng, shape, cuts, -0.22, 0.18) * values
    return jnp.clip(values, min=-most, max=most).astype(kind)


def setup_inputs(seed: int = 0) -> dict:
    seeds = jax.random.split(jax.random.key(seed), 7)
    return {
        "zonal_current": normal_values(seeds[0], (DEPTH_SHEETS, PARALLEL_TOTAL, MERIDIAN_TOTAL), 0.5, 6.0, ((1, 16), (2, 16)), jnp.float32),
        "meridian_current": normal_values(seeds[1], (DEPTH_SHEETS, PARALLEL_TOTAL, MERIDIAN_TOTAL), 0.5, 6.0, ((1, 16), (2, 16)), jnp.float32),
        "thermal_deviation": normal_values(seeds[2], (DEPTH_SHEETS, PARALLEL_TOTAL, MERIDIAN_TOTAL), 1.0, 6.0, ((1, 16), (2, 16)), jnp.float32),
        "saltiness_deviation": normal_values(seeds[3], (DEPTH_SHEETS, PARALLEL_TOTAL, MERIDIAN_TOTAL), 1.0, 6.0, ((1, 16), (2, 16)), jnp.float32),
        "dye_quantity": normal_values(seeds[4], (DEPTH_SHEETS, PARALLEL_TOTAL, MERIDIAN_TOTAL), 1.0, 6.0, ((1, 16), (2, 16)), jnp.float32),
        "water_indicator": draw_water_indicator(jax.random.fold_in(seeds[6], 71), 0),
    }


ADVECTION = 0.25
DIFFUSION = 0.2
PRESSURE_GAIN = 0.3
EXPAND_T = 0.4
EXPAND_S = 0.6
CORIOLIS_BASE = 0.1
CORIOLIS_SLOPE = 0.4


def coriolis(row_index, total_rows):
    mirrored = jnp.minimum(row_index, 2 * total_rows - 1 - row_index)
    return CORIOLIS_BASE + CORIOLIS_SLOPE * (mirrored.astype(jnp.float32) + 0.5) / total_rows


def advance(prognostic_bundle, sea, coriolis_rows):
    zonal = prognostic_bundle[0]
    meridional = prognostic_bundle[1]
    face_x = sea[:, 1:-1, 1:] * sea[:, 1:-1, :-1]
    face_y = sea[:, 1:, 1:-1] * sea[:, :-1, 1:-1]
    speed_x = 0.5 * (zonal[:, 1:-1, 1:] + zonal[:, 1:-1, :-1])
    speed_y = 0.5 * (meridional[:, 1:, 1:-1] + meridional[:, :-1, 1:-1])
    east_side = prognostic_bundle[:, :, 1:-1, 1:]
    west_side = prognostic_bundle[:, :, 1:-1, :-1]
    north_side = prognostic_bundle[:, :, 1:, 1:-1]
    south_side = prognostic_bundle[:, :, :-1, 1:-1]
    flux_x = face_x * (ADVECTION * speed_x * (0.5 * (east_side + west_side)) - DIFFUSION * (east_side - west_side))
    flux_y = face_y * (ADVECTION * speed_y * (0.5 * (north_side + south_side)) - DIFFUSION * (north_side - south_side))
    tendency = -((flux_x[..., 1:] - flux_x[..., :-1]) + (flux_y[..., 1:, :] - flux_y[..., :-1, :]))
    density = EXPAND_S * prognostic_bundle[3] - EXPAND_T * prognostic_bundle[2]
    pressure = jnp.cumsum(density, axis=0) - 0.5 * density
    grad_x = 0.5 * (face_x[:, :, 1:] * (pressure[:, 1:-1, 2:] - pressure[:, 1:-1, 1:-1]) + face_x[:, :, :-1] * (pressure[:, 1:-1, 1:-1] - pressure[:, 1:-1, :-2]))
    grad_y = 0.5 * (face_y[:, 1:, :] * (pressure[:, 2:, 1:-1] - pressure[:, 1:-1, 1:-1]) + face_y[:, :-1, :] * (pressure[:, 1:-1, 1:-1] - pressure[:, :-2, 1:-1]))
    centre = prognostic_bundle[:, :, 1:-1, 1:-1]
    spin = coriolis_rows[None, :, None]
    tend_u = tendency[0] + spin * centre[1] - PRESSURE_GAIN * grad_x
    tend_v = tendency[1] - spin * centre[0] - PRESSURE_GAIN * grad_y
    tendency = jnp.concatenate([tend_u[None], tend_v[None], tendency[2:]], axis=0)
    return sea[None, :, 1:-1, 1:-1] * (centre + tendency)


def wrap_fold(stacked_levels, flip_signs):
    extended = jnp.concatenate([stacked_levels[:, :, -1:], stacked_levels, stacked_levels[:, :, :1]], axis=2)
    upper_rows = flip_signs * extended[:, -1:, ::-1]
    lower_rows = jnp.zeros_like(extended[:, :1])
    return jnp.concatenate([lower_rows, extended, upper_rows], axis=1)


def reference(zonal_current, meridian_current, thermal_deviation, saltiness_deviation, dye_quantity, water_indicator):
    sea = water_indicator.astype(jnp.float32)
    flip_signs = jnp.repeat(jnp.array([-1.0, -1.0, 1.0, 1.0, 1.0], jnp.float32), DEPTH_SHEETS)[:, None, None]
    sea_ext = wrap_fold(sea, jnp.ones((DEPTH_SHEETS, 1, 1), jnp.float32))
    prognostic_bundle = jnp.stack([zonal_current, meridian_current, thermal_deviation, saltiness_deviation, dye_quantity], axis=0)
    coriolis_rows = coriolis(jnp.arange(PARALLEL_TOTAL), PARALLEL_TOTAL)
    for section in range(STEPS):
        extended = wrap_fold(prognostic_bundle.reshape(5 * DEPTH_SHEETS, PARALLEL_TOTAL, MERIDIAN_TOTAL), flip_signs).reshape(5, DEPTH_SHEETS, PARALLEL_TOTAL + 2, MERIDIAN_TOTAL + 2)
        prognostic_bundle = advance(extended, sea_ext, coriolis_rows)
    return (prognostic_bundle[0], prognostic_bundle[1], prognostic_bundle[2], prognostic_bundle[3], prognostic_bundle[4])
```

```python
import functools

import jax
import jax.numpy as jnp
from jax import lax
from jax.experimental import pallas as pl
from jax.experimental.pallas import tpu as pltpu
from jax.sharding import PartitionSpec as P

ADVECTION = 0.25
DIFFUSION = 0.2
PRESSURE_GAIN = 0.3
EXPAND_T = 0.4
EXPAND_S = 0.6
CORIOLIS_BASE = 0.1
CORIOLIS_SLOPE = 0.4

LEVELS = 4
UNROLL = 4
FIELDS = 5
ROWS = 32
COLS = 1024
Q_PLANES = FIELDS * LEVELS
M_AT = Q_PLANES
C_AT = Q_PLANES + LEVELS
PLANES = 2 * Q_PLANES + LEVELS
EDGE_PLANES = 4 * Q_PLANES + 3 * LEVELS
SPEED = ADVECTION * 0.25 / DIFFUSION
SLOPE = PRESSURE_GAIN * 0.5 / DIFFUSION

VMEM = pl.BlockSpec(memory_space=pltpu.VMEM)
ANY = pl.BlockSpec(memory_space=pl.ANY)
HBM = pl.BlockSpec(memory_space=pltpu.HBM)


def params(mib, **more):
    return pltpu.CompilerParams(vmem_limit_bytes=mib << 20, **more)


def f32(*shape):
    return jax.ShapeDtypeStruct(shape, jnp.float32)


def iota(dim, shape=(8, 128)):
    return lax.broadcasted_iota(jnp.int32, shape, dim)


def east(x):
    near = pltpu.roll(x, 127, 1)
    return jnp.where(iota(1) == 127, pltpu.roll(near, 7, 0), near)


def west(x):
    near = pltpu.roll(x, 1, 1)
    return jnp.where(iota(1) == 0, pltpu.roll(near, 1, 0), near)


def pressures(fields):
    total, out = None, []
    for k in range(LEVELS):
        density = EXPAND_S * fields[3 * LEVELS + k] - EXPAND_T * fields[2 * LEVELS + k]
        half = 0.5 * density
        out.append(half if total is None else total + half)
        total = density if total is None else total + density
    return out


def coriolis(row, total_rows):
    mirrored = jnp.minimum(row, 2 * total_rows - 1 - row)
    return CORIOLIS_BASE + CORIOLIS_SLOPE * (mirrored.astype(jnp.float32) + 0.5) / total_rows


def update_level(q, qe, qw, qn, qs, p, pe, pw, pn, ps, masks, spin):
    me, mw, mn, ms, m0 = masks
    ae = me * (SPEED * (q[0] + qe[0]))
    aw = mw * (SPEED * (q[0] + qw[0]))
    an = mn * (SPEED * (q[1] + qn[1]))
    a_s = ms * (SPEED * (q[1] + qs[1]))
    centre = m0 - ae + aw - an + a_s
    ke, kw, kn, ks = me - ae, mw + aw, mn - an, ms + a_s
    out = [
        centre * q[f] + ke * qe[f] + kw * qw[f] + kn * qn[f] + ks * qs[f] for f in range(FIELDS)
    ]
    gx = SLOPE * (me * (pe - p) + mw * (p - pw))
    gy = SLOPE * (mn * (pn - p) + ms * (p - ps))
    out[0] = out[0] + (spin * q[1] - gx)
    out[1] = out[1] - (spin * q[0] + gy)
    return out


def face_masks(m, m_e, m_w, m_n, m_s):
    scaled = DIFFUSION * m
    me, mw = scaled * m_e, scaled * m_w
    mn = jnp.zeros_like(m) if m_n is None else scaled * m_n
    ms = jnp.zeros_like(m) if m_s is None else scaled * m_s
    return me, mw, mn, ms, m - ((me + mw) + (mn + ms))


def pick(fields, k):
    return [fields[f * LEVELS + k] for f in range(FIELDS)]


def step_row(q, qn, qs, m, mn, ms, spin, add=None):
    p = pressures(q)
    pn, ps = pressures(qn), pressures(qs)
    out = [None] * Q_PLANES
    for k in range(LEVELS):
        own = pick(q, k)
        masks = face_masks(
            m[k],
            east(m[k]),
            west(m[k]),
            None if mn is None else mn[k],
            None if ms is None else ms[k],
        )
        new = update_level(
            own,
            [east(x) for x in own],
            [west(x) for x in own],
            pick(qn, k),
            pick(qs, k),
            p[k],
            east(p[k]),
            west(p[k]),
            pn[k],
            ps[k],
            masks,
            spin * m[k],
        )
        for f in range(FIELDS):
            i = f * LEVELS + k
            out[i] = new[f] if add is None else new[f] + add[i]
    return out


def row_of(ref, k, tile, r):
    return ref[k, tile, pl.ds(r, 8, stride=8), :]


def rows_kernel(*refs):
    args = refs[:6]
    msg_a, msg_b, scratch, floats, ints, sems = refs[6:]
    low, high, copies = [], [], []
    for side, rows in enumerate((low, high)):
        for f in range(6):
            here = floats.at[side, f] if f < FIELDS else ints.at[side]
            rows.append(here)
            two = pl.ds(6 * side, 2)
            tile = args[f].at[:, 3 * side, :, two, :]
            copies.append(pltpu.make_async_copy(tile, here.at[:, :, two, :], sems.at[side, f]))
    for copy in copies:
        copy.start()
    for copy in copies:
        copy.wait()
    lat = lax.axis_index("lat")
    last = lax.axis_size("lat") - 1
    odd = lax.rem(lat, 2) == 1

    def message(tiles, edge, inner, toward):
        q = [tiles[f][k, :, edge, :] for f in range(FIELDS) for k in range(LEVELS)]
        n = [tiles[f][k, :, inner, :] for f in range(FIELDS) for k in range(LEVELS)]
        m = [tiles[5][k, :, edge, :].astype(jnp.float32) for k in range(LEVELS)]
        mi = [tiles[5][k, :, inner, :].astype(jnp.float32) for k in range(LEVELS)]
        p, pi = pressures(q), pressures(n)
        brought = [None] * Q_PLANES
        for k in range(LEVELS):
            mask = DIFFUSION * (m[k] * mi[k])
            a = mask * (SPEED * (q[LEVELS + k] + n[LEVELS + k])) * toward
            ki, ko = mask + a, a - mask
            for f in range(FIELDS):
                i = f * LEVELS + k
                brought[i] = ki * n[i] + ko * q[i]
            i = LEVELS + k
            brought[i] = brought[i] - toward * (SLOPE * mask * (p[k] - pi[k]))
        return q + m + brought

    top = message(high, 7, 6, 1.0)
    bottom = message(low, 0, 1, -1.0)
    for i in range(PLANES):
        msg_a[pl.ds(8 * i, 8), :] = jnp.where(odd, bottom[i], top[i])
        msg_b[pl.ds(8 * i, 8), :] = jnp.where(odd, top[i], bottom[i])

    @pl.when(lat == last)
    def _():
        lane = iota(1)
        for i in range(PLANES):
            x = jnp.take_along_axis(top[i], 127 - lane, axis=1)
            flip = i < 2 * LEVELS or C_AT <= i < C_AT + 2 * LEVELS
            scratch[pl.ds(8 * i, 8), :] = -x if flip else x
        for s in range(8):
            msg_b[pl.ds(7 - s, PLANES, stride=8), :] = scratch[pl.ds(s, PLANES, stride=8), :]


def inner_kernel(*refs):
    args, outs = refs[:6], refs[6:11]
    edge, cols = refs[11:13]
    floats, ints, ready, first, second, mask, press, faces, sems, out_sems = refs[13:]
    lat = lax.axis_index("lat")
    total = ROWS * lax.axis_size("lat")
    base = lat * ROWS
    lane = iota(1)

    def at(row, per_row, i, off=0):
        start = pl.multiple_of(8 * (row * per_row + i + 1), 8)
        return pl.ds(start + off, 8)

    def beside(ref, row, per_row, i):
        x = ref[at(row, per_row, i), :]
        after = ref[at(row, per_row, i, 1), :]
        before = ref[at(row, per_row, i, -1), :]
        e = pltpu.roll(jnp.where(lane == 0, after, x), 127, 1)
        w = pltpu.roll(jnp.where(lane == 127, before, x), 1, 1)
        return x, e, w

    def fetch(tile):
        return [
            pltpu.make_async_copy(
                args[f].at[:, tile],
                floats.at[tile, f] if f < FIELDS else ints.at[tile],
                sems.at[tile, f],
            )
            for f in range(6)
        ]

    def put(tile):
        return [
            pltpu.make_async_copy(ready.at[tile, f], outs[f].at[:, tile], out_sems.at[tile, f])
            for f in range(FIELDS)
        ]

    def step(source, s, r):
        spin = coriolis(base + r, total)
        levels = []
        for k in range(LEVELS):
            sides = [beside(source, r, Q_PLANES, f * LEVELS + k) for f in range(FIELDS)]
            p, pe, pw = beside(press.at[s], r, LEVELS, k)
            if s == 0:
                m, me, mw = beside(mask, r, LEVELS, k)
                mn, ms = mask[at(r + 1, LEVELS, k), :], mask[at(r - 1, LEVELS, k), :]
                face = face_masks(m, me, mw, mn, ms)
                for i in range(5):
                    faces[r, k, i] = face[i]
            else:
                m = mask[at(r, LEVELS, k), :]
                face = [faces[r, k, i] for i in range(5)]
            new = update_level(
                [x[0] for x in sides],
                [x[1] for x in sides],
                [x[2] for x in sides],
                [source[at(r + 1, Q_PLANES, f * LEVELS + k), :] for f in range(FIELDS)],
                [source[at(r - 1, Q_PLANES, f * LEVELS + k), :] for f in range(FIELDS)],
                p,
                pe,
                pw,
                press[s, at(r + 1, LEVELS, k), :],
                press[s, at(r - 1, LEVELS, k), :],
                face,
                spin * m,
            )
            levels.append(new)
        return [levels[k][f] for f in range(FIELDS) for k in range(LEVELS)]

    def step_one(r, c):
        new = step(first, 0, r)
        for i in range(Q_PLANES):
            second[at(r, Q_PLANES, i), :] = new[i]
        for k, p in enumerate(pressures(new)):
            press[1, at(r, LEVELS, k), :] = p
        return c

    def step_two(r, c):
        new = step(second, 1, r)
        tile = r // 8
        for f in range(FIELDS):
            for k in range(LEVELS):
                ready[tile, f, k, pl.ds(r % 8, 8, stride=8), :] = new[f * LEVELS + k]
        return c

    for tile in range(4):
        for copy in fetch(tile):
            copy.start()

    for tile in range(4):
        for copy in fetch(tile):
            copy.wait()
        for r8 in range(8):
            r = tile * 8 + r8
            q = []
            for f in range(FIELDS):
                for k in range(LEVELS):
                    x = floats[tile, f, k, pl.ds(r8, 8, stride=8), :]
                    first[at(r, Q_PLANES, f * LEVELS + k), :] = x
                    q.append(x)
            p = pressures(q)
            for k in range(LEVELS):
                m = ints[tile, k, pl.ds(r8, 8, stride=8), :].astype(jnp.float32)
                mask[at(r, LEVELS, k), :] = m
                press[0, at(r, LEVELS, k), :] = p[k]
        lax.fori_loop(max(1, 8 * tile - 1), 8 * tile + 7, step_one, 0, unroll=UNROLL)
        lax.fori_loop(max(2, 8 * tile - 2), 8 * tile + 6, step_two, 0, unroll=UNROLL)
        if tile > 0:
            for copy in put(tile - 1):
                copy.start()
    for copy in put(3):
        copy.start()

    big_lane = iota(1, (128, 128))
    for f in range(6):
        tiles = [floats.at[t, f] if f < FIELDS else ints.at[t] for t in range(4)]
        left = [tiles[t][k, pl.ds(0, 8), :] for k in range(LEVELS) for t in range(4)]
        right = [tiles[t][k, pl.ds(56, 8), :] for k in range(LEVELS) for t in range(4)]
        left = jnp.concatenate(left, axis=0).astype(jnp.float32)
        right = jnp.concatenate(right, axis=0).astype(jnp.float32)
        both = jnp.where(big_lane < 4, left, pltpu.roll(right, 8, 1))
        cols[f] = both.T[:8]

    for side in range(2):
        e = 0 if side == 0 else ROWS - 1
        d = 1 if side == 0 else -1
        for i in range(Q_PLANES):
            edge[side, i] = first[at(e, Q_PLANES, i), :]
            edge[side, Q_PLANES + i] = first[at(e + d, Q_PLANES, i), :]
            edge[side, 2 * Q_PLANES + i] = second[at(e + d, Q_PLANES, i), :]
            edge[side, 3 * Q_PLANES + i] = second[at(e + 2 * d, Q_PLANES, i), :]
        for k in range(LEVELS):
            for j in range(3):
                edge[side, 4 * Q_PLANES + j * LEVELS + k] = mask[at(e + j * d, LEVELS, k), :]

    for tile in range(4):
        for copy in put(tile):
            copy.wait()


def columns_kernel(recv_a, recv_b, cols, msg_a, msg_b, halos):
    lat_odd = lax.rem(lax.axis_index("lat"), 2) == 1
    lon_odd = lax.rem(lax.axis_index("lon"), 2) == 1
    lane = iota(1, (PLANES, 128))

    def edges(ref):
        left = ref[pl.ds(0, PLANES, stride=8), :]
        right = ref[pl.ds(7, PLANES, stride=8), :]
        return jnp.where(lane < 4, left, pltpu.roll(right, 8, 1))

    from_a, from_b = edges(recv_a), edges(recv_b)
    south = jnp.where(lat_odd, from_a, from_b)
    north = jnp.where(lat_odd, from_b, from_a)
    gap = jnp.zeros((64 - PLANES, 128), jnp.float32)
    turned = jnp.concatenate([south, gap, north, gap], axis=0).T[:8]
    halo_s = turned
    halo_n = pltpu.roll(turned, 64, 1)
    halos[0] = halo_s
    halos[1] = halo_n
    sub = iota(0)

    def pack(at, corner):
        parts = []
        for group in range(2):
            x = jnp.zeros((8, 128), jnp.float32)
            for j in range(4):
                f = group * 4 + j
                if f < 6:
                    y = pltpu.roll(cols[f], (2 * j - at) % 8, 0)
                    x = jnp.where(sub // 2 == j, y, x)
            parts.append(x)
        parts[1] = jnp.where(sub == 4, pltpu.roll(halo_s, (4 - corner) % 8, 0), parts[1])
        parts[1] = jnp.where(sub == 5, pltpu.roll(halo_n, (5 - corner) % 8, 0), parts[1])
        return parts

    westward, eastward = pack(0, 0), pack(6, 7)
    for g in range(2):
        msg_a[pl.ds(8 * g, 8), :] = jnp.where(lon_odd, westward[g], eastward[g])
        msg_b[pl.ds(8 * g, 8), :] = jnp.where(lon_odd, eastward[g], westward[g])


def border_kernel(*refs):
    recv_a, recv_b, edge = refs[:3]
    tiles, outs = refs[3:8], refs[8:13]
    side = pl.program_id(0)
    lat = lax.axis_index("lat")
    odd = lax.rem(lat, 2) == 1
    total = ROWS * lax.axis_size("lat")
    base = lat * ROWS
    for f in range(FIELDS):
        outs[f][...] = tiles[f][...]

    def run(low):
        e = 0 if low else ROWS - 1
        d = 1 if low else -1
        s = 0 if low else 1
        take_a = odd if low else jnp.logical_not(odd)
        halo = [
            jnp.where(take_a, recv_a[pl.ds(8 * i, 8), :], recv_b[pl.ds(8 * i, 8), :])
            for i in range(PLANES)
        ]
        q_out, m_out, add = halo[:M_AT], halo[M_AT:C_AT], halo[C_AT:]
        q0 = [edge[s, i] for i in range(Q_PLANES)]
        q1 = [edge[s, Q_PLANES + i] for i in range(Q_PLANES)]
        m0, m1, m2 = (
            [edge[s, 4 * Q_PLANES + j * LEVELS + k] for k in range(LEVELS)] for j in range(3)
        )

        def row(q, inward, outward, m, m_in, m_o, at, extra=None):
            spin = coriolis(base + at, total)
            if low:
                return step_row(q, inward, outward, m, m_in, m_o, spin, extra)
            return step_row(q, outward, inward, m, m_o, m_in, spin, extra)

        n_out = row(q_out, q0, q_out, m_out, m0, None, e - d, add)
        n0 = row(q0, q1, q_out, m0, m1, m_out, e)
        n1 = [edge[s, 2 * Q_PLANES + i] for i in range(Q_PLANES)]
        n2 = [edge[s, 3 * Q_PLANES + i] for i in range(Q_PLANES)]
        r0 = row(n0, n1, n_out, m0, m1, m_out, e)
        r1 = row(n1, n2, n0, m1, m2, m0, e + d)
        for f in range(FIELDS):
            for k in range(LEVELS):
                i = f * LEVELS + k
                outs[f][k, 0, pl.ds(e % 8, 8, stride=8), :] = r0[i]
                outs[f][k, 0, pl.ds((e + d) % 8, 8, stride=8), :] = r1[i]

    @pl.when(side == 0)
    def _():
        run(True)

    @pl.when(side == 1)
    def _():
        run(False)


def seam_kernel(*refs):
    recv_a, recv_b, cols, halos = refs[:4]
    outs = refs[9:14]
    left, right, sems = refs[14:]
    loads = []
    for f in range(FIELDS):
        loads.append(pltpu.make_async_copy(outs[f].at[:, :, pl.ds(0, 8), :], left.at[f], sems.at[f]))
        loads.append(
            pltpu.make_async_copy(
                outs[f].at[:, :, pl.ds(56, 8), :], right.at[f], sems.at[FIELDS + f]
            )
        )
    for copy in loads:
        copy.start()

    lon_odd = lax.rem(lax.axis_index("lon"), 2) == 1
    lat = lax.axis_index("lat")
    total = ROWS * lax.axis_size("lat")
    sub, lane = iota(0), iota(1)
    pa = [recv_a[pl.ds(8 * g, 8), :] for g in range(2)]
    pb = [recv_b[pl.ds(8 * g, 8), :] for g in range(2)]
    from_west = [jnp.where(lon_odd, a, b) for a, b in zip(pa, pb)]
    from_east = [jnp.where(lon_odd, b, a) for a, b in zip(pa, pb)]

    h_s, h_n = halos[0], halos[1]
    rim = []
    for g, h in enumerate((h_s, h_n)):
        w = jnp.where(sub == 1, pltpu.roll(from_west[1], (1 - 4 - g) % 8, 0), pltpu.roll(h, 2, 0))
        e = jnp.where(sub == 6, pltpu.roll(from_east[1], (6 - 4 - g) % 8, 0), pltpu.roll(h, 6, 0))
        rim.append((w, e))

    spots = ((0, 0, 0), (33, 1, 0), (64, 0, 1), (97, 1, 1))

    def at_rims(base, plane):
        x = base
        for spot, g, side in spots:
            x = jnp.where(lane == spot, pltpu.roll(rim[g][side], (spot - plane) % 128, 1), x)
        return x

    def spread(f, k):
        group, j = f // 4, f % 4
        own = cols[f]
        w = pltpu.roll(from_west[group], (6 - 2 * j) % 8, 0)
        e = pltpu.roll(from_east[group], (8 - 2 * j) % 8, 0)
        w = pltpu.roll(jnp.where(sub >= 6, w, own), 2, 0)
        e = pltpu.roll(jnp.where(sub < 2, e, own), 6, 0)
        x = jnp.where(
            lane < 64,
            pltpu.roll(w, (1 - 32 * k) % 128, 1),
            pltpu.roll(e, (65 - 32 * k) % 128, 1),
        )
        return at_rims(x, f * LEVELS + k)

    q = [spread(f, k) for f in range(FIELDS) for k in range(LEVELS)]
    row = lax.rem(lane, 64) - 1
    valid = row <= ROWS
    m = [jnp.where(valid, spread(5, k), 0.0) for k in range(LEVELS)]
    zero = jnp.zeros((8, 128), jnp.float32)
    brought = [at_rims(zero, C_AT + i) for i in range(Q_PLANES)]
    spin = coriolis(row + lat * ROWS, total)

    def move(x, d, axis):
        return pltpu.roll(x, d % x.shape[axis], axis)

    def shifted(x):
        return move(x, -1, 0), move(x, 1, 0), move(x, -1, 1), move(x, 1, 1)

    masks = [face_masks(m[k], *shifted(m[k])) for k in range(LEVELS)]
    for s in range(2):
        p = pressures(q)
        new_q = [None] * Q_PLANES
        for k in range(LEVELS):
            own = pick(q, k)
            sides = [shifted(x) for x in own]
            qe, qw, qn, qs = ([x[i] for x in sides] for i in range(4))
            new = update_level(own, qe, qw, qn, qs, p[k], *shifted(p[k]), masks[k], spin * m[k])
            for f in range(FIELDS):
                i = f * LEVELS + k
                new_q[i] = new[f] + brought[i] if s == 0 else new[f]
        q = new_q

    for copy in loads:
        copy.wait()

    big_lane = iota(1, (128, 128))
    gap = jnp.zeros((112, 128), jnp.float32)
    for f in range(FIELDS):
        w, e = zero, zero
        for k in range(LEVELS):
            x = q[f * LEVELS + k]
            here = lane // 32 == k
            w = jnp.where(here, pltpu.roll(x, (32 * k - 1) % 128, 1), w)
            e = jnp.where(here, pltpu.roll(x, (32 * k - 65) % 128, 1), e)
        w, e = pltpu.roll(w, 6, 0), pltpu.roll(e, 2, 0)
        turned = jnp.concatenate([w, gap, e], axis=0).T
        a = left[f].reshape(128, 128)
        b = right[f].reshape(128, 128)
        left[f] = jnp.where(big_lane < 2, turned, a).reshape(LEVELS, 4, 8, 128)
        right[f] = jnp.where(big_lane >= 126, turned, b).reshape(LEVELS, 4, 8, 128)

    stores = []
    for f in range(FIELDS):
        stores.append(pltpu.make_async_copy(left.at[f], outs[f].at[:, :, pl.ds(0, 8), :], sems.at[f]))
        stores.append(
            pltpu.make_async_copy(
                right.at[f], outs[f].at[:, :, pl.ds(56, 8), :], sems.at[FIELDS + f]
            )
        )
    for copy in stores:
        copy.start()
    for copy in stores:
        copy.wait()


def view(x):
    return x.reshape(LEVELS, 4, 8, 8, 128).transpose(0, 1, 3, 2, 4)


def unview(x):
    return x.reshape(LEVELS, 4, 8, 8, 128).transpose(0, 1, 3, 2, 4).reshape(LEVELS, ROWS, COLS)


def routes(lons, lats):
    def at(lon, lat):
        return lon * lats + lat

    def other(i, count, shift):
        return ((i + shift) ^ 1) - shift

    lat_a, lat_b, lon_a, lon_b = [], [], [], []
    for lon in range(lons):
        for lat in range(lats):
            me = at(lon, lat)
            lat_a.append((me, at(lon, lat ^ 1)))
            if lat == lats - 1:
                lat_b.append((me, at(lons - 1 - lon, lat)))
            elif lat > 0:
                lat_b.append((me, at(lon, other(lat, lats, 1))))
            lon_a.append((me, at(lon ^ 1, lat)))
            lon_b.append((me, at(other(lon, lons, 1) % lons, lat)))
    return lat_a, lat_b, lon_a, lon_b


def inner_call(args):
    return pl.pallas_call(
        inner_kernel,
        in_specs=[HBM] * 6,
        out_specs=[HBM] * FIELDS + [VMEM] * 2,
        out_shape=[f32(LEVELS, 4, 64, 128)] * FIELDS
        + [f32(2, EDGE_PLANES, 8, 128), f32(6, 8, 128)],
        scratch_shapes=[
            pltpu.VMEM((4, FIELDS, LEVELS, 64, 128), jnp.float32),
            pltpu.VMEM((4, LEVELS, 64, 128), jnp.int32),
            pltpu.VMEM((4, FIELDS, LEVELS, 64, 128), jnp.float32),
            pltpu.VMEM((8 * (ROWS * Q_PLANES + 2), 128), jnp.float32),
            pltpu.VMEM((8 * (ROWS * Q_PLANES + 2), 128), jnp.float32),
            pltpu.VMEM((8 * (ROWS * LEVELS + 2), 128), jnp.float32),
            pltpu.VMEM((2, 8 * (ROWS * LEVELS + 2), 128), jnp.float32),
            pltpu.VMEM((ROWS, LEVELS, 5, 8, 128), jnp.float32),
            pltpu.SemaphoreType.DMA((4, 6)),
            pltpu.SemaphoreType.DMA((4, FIELDS)),
        ],
        compiler_params=params(62),
        cost_estimate=pl.CostEstimate(flops=26 << 20, bytes_accessed=6 << 20, transcendentals=0),
        name="inner_rows",
    )(*args)


def per_device(*args):
    axes = ("lon", "lat")
    lat_a, lat_b, lon_a, lon_b = routes(lax.axis_size("lon"), lax.axis_size("lat"))
    args = [view(x) for x in args]
    out = f32(LEVELS, 4, 64, 128)
    planes = EDGE_PLANES

    send_a, send_b = pl.pallas_call(
        rows_kernel,
        in_specs=[HBM] * 6,
        out_specs=[VMEM] * 2,
        out_shape=[f32(PLANES * 8, 128)] * 2,
        scratch_shapes=[
            pltpu.VMEM((PLANES * 8, 128), jnp.float32),
            pltpu.VMEM((2, FIELDS, LEVELS, 8, 8, 128), jnp.float32),
            pltpu.VMEM((2, LEVELS, 8, 8, 128), jnp.int32),
            pltpu.SemaphoreType.DMA((2, 6)),
        ],
        compiler_params=params(63),
        cost_estimate=pl.CostEstimate(flops=1 << 20, bytes_accessed=2 << 20, transcendentals=0),
        name="edge_rows",
    )(*args)
    args = [x.reshape(LEVELS, 4, 64, 128) for x in args]
    recv_b = lax.ppermute(send_b, axes, lat_b)
    recv_a = lax.ppermute(send_a, axes, lat_a)

    *inner, edge, cols = inner_call(args)

    send_la, send_lb, halos = pl.pallas_call(
        columns_kernel,
        in_specs=[VMEM] * 3,
        out_specs=[VMEM] * 3,
        out_shape=[f32(16, 128), f32(16, 128), f32(2, 8, 128)],
        compiler_params=params(16),
        name="edge_columns",
    )(recv_a, recv_b, cols)
    recv_lb = lax.ppermute(send_lb, axes, lon_b)
    recv_la = lax.ppermute(send_la, axes, lon_a)

    whole2 = pl.BlockSpec((PLANES * 8, 128), lambda i: (0, 0))
    all_edges = pl.BlockSpec((2, planes, 8, 128), lambda i: (0, 0, 0, 0))
    sides = pl.BlockSpec((LEVELS, 1, 64, 128), lambda i: (0, 3 * i, 0, 0))
    border = pl.pallas_call(
        border_kernel,
        grid=(2,),
        in_specs=[whole2, whole2, all_edges] + [sides] * FIELDS,
        out_specs=[sides] * FIELDS,
        out_shape=[out] * FIELDS,
        input_output_aliases={3 + f: f for f in range(FIELDS)},
        compiler_params=params(24),
        cost_estimate=pl.CostEstimate(flops=4 << 20, bytes_accessed=4 << 20, transcendentals=0),
        name="border_rows",
    )(recv_a, recv_b, edge, *inner)

    final = pl.pallas_call(
        seam_kernel,
        in_specs=[VMEM] * 4 + [ANY] * FIELDS,
        out_specs=[ANY] * FIELDS,
        out_shape=[out] * FIELDS,
        input_output_aliases={4 + f: f for f in range(FIELDS)},
        scratch_shapes=[
            pltpu.VMEM((FIELDS, LEVELS, 4, 8, 128), jnp.float32),
            pltpu.VMEM((FIELDS, LEVELS, 4, 8, 128), jnp.float32),
            pltpu.SemaphoreType.DMA((2 * FIELDS,)),
        ],
        compiler_params=params(16),
        name="seam_columns",
    )(recv_la, recv_lb, cols, halos, *border)
    return tuple(unview(x) for x in final)


def solution(mesh):
    spec = P(None, "lat", "lon")
    return jax.shard_map(
        per_device,
        mesh=mesh,
        in_specs=(spec,) * 6,
        out_specs=(spec,) * 5,
        check_vma=False,
    )
```

```python
import functools

import jax
import jax.numpy as jnp
from jax import lax
from jax.experimental import pallas as pl
from jax.experimental.pallas import tpu as pltpu
from jax.sharding import PartitionSpec as P

ADVECTION = 0.25
DIFFUSION = 0.2
PRESSURE_GAIN = 0.3
EXPAND_T = 0.4
EXPAND_S = 0.6
CORIOLIS_BASE = 0.1
CORIOLIS_SLOPE = 0.4

LEVELS = 4
UNROLL = 8
LIMIT = 50.3
FIELDS = 5
ROWS = 32
COLS = 1024
Q_PLANES = FIELDS * LEVELS
M_AT = Q_PLANES
C_AT = Q_PLANES + LEVELS
PLANES = 2 * Q_PLANES + LEVELS
EDGE_PLANES = 4 * Q_PLANES + 3 * LEVELS
SPEED = ADVECTION * 0.25 / DIFFUSION
SLOPE = PRESSURE_GAIN * 0.5 / DIFFUSION

VMEM = pl.BlockSpec(memory_space=pltpu.VMEM)
HBM = pl.BlockSpec(memory_space=pltpu.HBM)


def params(mib, **more):
    return pltpu.CompilerParams(vmem_limit_bytes=int(mib * (1 << 20)), **more)


def f32(*shape):
    return jax.ShapeDtypeStruct(shape, jnp.float32)


def iota(dim, shape=(8, 128)):
    return lax.broadcasted_iota(jnp.int32, shape, dim)


def east(x):
    near = pltpu.roll(x, 127, 1)
    return jnp.where(iota(1) == 127, pltpu.roll(near, 7, 0), near)


def west(x):
    near = pltpu.roll(x, 1, 1)
    return jnp.where(iota(1) == 0, pltpu.roll(near, 1, 0), near)


def pressures(fields):
    total, out = None, []
    for k in range(LEVELS):
        density = EXPAND_S * fields[3 * LEVELS + k] - EXPAND_T * fields[2 * LEVELS + k]
        half = 0.5 * density
        out.append(half if total is None else total + half)
        total = density if total is None else total + density
    return out


def coriolis(row, total_rows):
    mirrored = jnp.minimum(row, 2 * total_rows - 1 - row)
    return CORIOLIS_BASE + CORIOLIS_SLOPE * (mirrored.astype(jnp.float32) + 0.5) / total_rows


def update_level(q, qe, qw, qn, qs, p, pe, pw, pn, ps, masks, spin):
    me, mw, mn, ms, m0 = masks
    ae = me * (SPEED * (q[0] + qe[0]))
    aw = mw * (SPEED * (q[0] + qw[0]))
    an = mn * (SPEED * (q[1] + qn[1]))
    a_s = ms * (SPEED * (q[1] + qs[1]))
    centre = m0 - ae + aw - an + a_s
    ke, kw, kn, ks = me - ae, mw + aw, mn - an, ms + a_s
    out = [
        centre * q[f] + ke * qe[f] + kw * qw[f] + kn * qn[f] + ks * qs[f] for f in range(FIELDS)
    ]
    gx = SLOPE * (me * (pe - p) + mw * (p - pw))
    gy = SLOPE * (mn * (pn - p) + ms * (p - ps))
    out[0] = out[0] + (spin * q[1] - gx)
    out[1] = out[1] - (spin * q[0] + gy)
    return out


def face_masks(m, m_e, m_w, m_n, m_s):
    scaled = DIFFUSION * m
    me, mw = scaled * m_e, scaled * m_w
    mn = jnp.zeros_like(m) if m_n is None else scaled * m_n
    ms = jnp.zeros_like(m) if m_s is None else scaled * m_s
    return me, mw, mn, ms, m - ((me + mw) + (mn + ms))


def pick(fields, k):
    return [fields[f * LEVELS + k] for f in range(FIELDS)]


def step_row(q, qn, qs, m, mn, ms, spin, add=None):
    p = pressures(q)
    pn, ps = pressures(qn), pressures(qs)
    out = [None] * Q_PLANES
    for k in range(LEVELS):
        own = pick(q, k)
        masks = face_masks(
            m[k],
            east(m[k]),
            west(m[k]),
            None if mn is None else mn[k],
            None if ms is None else ms[k],
        )
        new = update_level(
            own,
            [east(x) for x in own],
            [west(x) for x in own],
            pick(qn, k),
            pick(qs, k),
            p[k],
            east(p[k]),
            west(p[k]),
            pn[k],
            ps[k],
            masks,
            spin * m[k],
        )
        for f in range(FIELDS):
            i = f * LEVELS + k
            out[i] = new[f] if add is None else new[f] + add[i]
    return out


def row_of(ref, k, tile, r):
    return ref[k, tile, pl.ds(r, 8, stride=8), :]


def rows_kernel(*refs):
    args = refs[:6]
    msg_a, msg_b = refs[6:8]
    kept = refs[8:14]
    scratch, sems = refs[14:]
    copies = [
        [
            pltpu.make_async_copy(args[f].at[:, t], kept[f].at[:, t], sems.at[t, f])
            for f in range(6)
        ]
        for t in range(4)
    ]
    for t in (0, 3, 1, 2):
        for copy in copies[t]:
            copy.start()
    for t in (0, 3):
        for copy in copies[t]:
            copy.wait()
    low, high = ([x.at[:, t] for x in kept] for t in (0, 3))
    lat = lax.axis_index("lat")
    last = lax.axis_size("lat") - 1
    odd = lax.rem(lat, 2) == 1

    def message(tiles, edge, inner, toward):
        q = [tiles[f][k, :, edge, :] for f in range(FIELDS) for k in range(LEVELS)]
        n = [tiles[f][k, :, inner, :] for f in range(FIELDS) for k in range(LEVELS)]
        m = [tiles[5][k, :, edge, :].astype(jnp.float32) for k in range(LEVELS)]
        mi = [tiles[5][k, :, inner, :].astype(jnp.float32) for k in range(LEVELS)]
        p, pi = pressures(q), pressures(n)
        brought = [None] * Q_PLANES
        for k in range(LEVELS):
            mask = DIFFUSION * (m[k] * mi[k])
            a = mask * (SPEED * (q[LEVELS + k] + n[LEVELS + k])) * toward
            ki, ko = mask + a, a - mask
            for f in range(FIELDS):
                i = f * LEVELS + k
                brought[i] = ki * n[i] + ko * q[i]
            i = LEVELS + k
            brought[i] = brought[i] - toward * (SLOPE * mask * (p[k] - pi[k]))
        return q + m + brought

    top = message(high, 7, 6, 1.0)
    bottom = message(low, 0, 1, -1.0)
    for i in range(PLANES):
        msg_a[pl.ds(8 * i, 8), :] = jnp.where(odd, bottom[i], top[i])
        msg_b[pl.ds(8 * i, 8), :] = jnp.where(odd, top[i], bottom[i])

    @pl.when(lat == last)
    def _():
        lane = iota(1)
        for i in range(PLANES):
            x = jnp.take_along_axis(top[i], 127 - lane, axis=1)
            flip = i < 2 * LEVELS or C_AT <= i < C_AT + 2 * LEVELS
            scratch[pl.ds(8 * i, 8), :] = -x if flip else x
        for s in range(8):
            msg_b[pl.ds(7 - s, PLANES, stride=8), :] = scratch[pl.ds(s, PLANES, stride=8), :]

    for t in (1, 2):
        for copy in copies[t]:
            copy.wait()


def inner_kernel(*refs):
    args, outs = refs[:6], refs[6:11]
    edge, cols = refs[11:13]
    ready, first, second, mask, press, faces, out_sems = refs[13:]
    lat = lax.axis_index("lat")
    total = ROWS * lax.axis_size("lat")
    base = lat * ROWS
    lane = iota(1)

    def at(row, per_row, i, off=0):
        start = pl.multiple_of(8 * (row * per_row + i + 1), 8)
        return pl.ds(start + off, 8)

    def beside(ref, row, per_row, i):
        x = ref[at(row, per_row, i), :]
        after = ref[at(row, per_row, i, 1), :]
        before = ref[at(row, per_row, i, -1), :]
        e = pltpu.roll(jnp.where(lane == 0, after, x), 127, 1)
        w = pltpu.roll(jnp.where(lane == 127, before, x), 1, 1)
        return x, e, w

    def put(tile):
        return [
            pltpu.make_async_copy(ready.at[tile, f], outs[f].at[:, tile], out_sems.at[tile, f])
            for f in range(FIELDS)
        ]

    def step(source, s, r):
        spin = coriolis(base + r, total)
        levels = []
        for k in range(LEVELS):
            sides = [beside(source, r, Q_PLANES, f * LEVELS + k) for f in range(FIELDS)]
            p, pe, pw = beside(press.at[s], r, LEVELS, k)
            if s == 0:
                m, me, mw = beside(mask, r, LEVELS, k)
                mn, ms = mask[at(r + 1, LEVELS, k), :], mask[at(r - 1, LEVELS, k), :]
                face = face_masks(m, me, mw, mn, ms)
                for i in range(5):
                    faces[r, k, i] = face[i]
            else:
                m = mask[at(r, LEVELS, k), :]
                face = [faces[r, k, i] for i in range(5)]
            new = update_level(
                [x[0] for x in sides],
                [x[1] for x in sides],
                [x[2] for x in sides],
                [source[at(r + 1, Q_PLANES, f * LEVELS + k), :] for f in range(FIELDS)],
                [source[at(r - 1, Q_PLANES, f * LEVELS + k), :] for f in range(FIELDS)],
                p,
                pe,
                pw,
                press[s, at(r + 1, LEVELS, k), :],
                press[s, at(r - 1, LEVELS, k), :],
                face,
                spin * m,
            )
            levels.append(new)
        return [levels[k][f] for f in range(FIELDS) for k in range(LEVELS)]

    def step_one(r, c):
        new = step(first, 0, r)
        for i in range(Q_PLANES):
            second[at(r, Q_PLANES, i), :] = new[i]
        for k, p in enumerate(pressures(new)):
            press[1, at(r, LEVELS, k), :] = p
        return c

    def step_two(r, c):
        new = step(second, 1, r)
        tile = r // 8
        for f in range(FIELDS):
            for k in range(LEVELS):
                ready[tile, f, k, pl.ds(r % 8, 8, stride=8), :] = new[f * LEVELS + k]
        return c

    for tile in range(4):
        for r8 in range(8):
            r = tile * 8 + r8
            q = []
            for f in range(FIELDS):
                for k in range(LEVELS):
                    x = row_of(args[f], k, tile, r8)
                    first[at(r, Q_PLANES, f * LEVELS + k), :] = x
                    q.append(x)
            p = pressures(q)
            for k in range(LEVELS):
                m = row_of(args[5], k, tile, r8).astype(jnp.float32)
                mask[at(r, LEVELS, k), :] = m
                press[0, at(r, LEVELS, k), :] = p[k]
        lax.fori_loop(max(1, 8 * tile - 1), 8 * tile + 7, step_one, 0, unroll=UNROLL)
        lax.fori_loop(max(2, 8 * tile - 2), 8 * tile + 6, step_two, 0, unroll=UNROLL)
        if tile > 0:
            for copy in put(tile - 1):
                copy.start()
    for copy in put(3):
        copy.start()

    big_lane = iota(1, (128, 128))
    for f in range(6):
        left = args[f][:, :, pl.ds(0, 8), :].reshape(128, 128).astype(jnp.float32)
        right = args[f][:, :, pl.ds(56, 8), :].reshape(128, 128).astype(jnp.float32)
        both = jnp.where(big_lane < 4, left, pltpu.roll(right, 8, 1))
        cols[f] = both.T[:8]

    for side in range(2):
        e = 0 if side == 0 else ROWS - 1
        d = 1 if side == 0 else -1
        for i in range(Q_PLANES):
            edge[side, i] = first[at(e, Q_PLANES, i), :]
            edge[side, Q_PLANES + i] = first[at(e + d, Q_PLANES, i), :]
            edge[side, 2 * Q_PLANES + i] = second[at(e + d, Q_PLANES, i), :]
            edge[side, 3 * Q_PLANES + i] = second[at(e + 2 * d, Q_PLANES, i), :]
        for k in range(LEVELS):
            for j in range(3):
                edge[side, 4 * Q_PLANES + j * LEVELS + k] = mask[at(e + j * d, LEVELS, k), :]

    for tile in range(4):
        for copy in put(tile):
            copy.wait()


def columns_kernel(recv_a, recv_b, cols, msg_a, msg_b, halos):
    lat_odd = lax.rem(lax.axis_index("lat"), 2) == 1
    lon_odd = lax.rem(lax.axis_index("lon"), 2) == 1
    lane = iota(1, (PLANES, 128))

    def edges(ref):
        left = ref[pl.ds(0, PLANES, stride=8), :]
        right = ref[pl.ds(7, PLANES, stride=8), :]
        return jnp.where(lane < 4, left, pltpu.roll(right, 8, 1))

    from_a, from_b = edges(recv_a), edges(recv_b)
    south = jnp.where(lat_odd, from_a, from_b)
    north = jnp.where(lat_odd, from_b, from_a)
    gap = jnp.zeros((64 - PLANES, 128), jnp.float32)
    turned = jnp.concatenate([south, gap, north, gap], axis=0).T[:8]
    halo_s = turned
    halo_n = pltpu.roll(turned, 64, 1)
    halos[0] = halo_s
    halos[1] = halo_n
    sub = iota(0)

    def pack(at, corner):
        parts = []
        for group in range(2):
            x = jnp.zeros((8, 128), jnp.float32)
            for j in range(4):
                f = group * 4 + j
                if f < 6:
                    y = pltpu.roll(cols[f], (2 * j - at) % 8, 0)
                    x = jnp.where(sub // 2 == j, y, x)
            parts.append(x)
        parts[1] = jnp.where(sub == 4, pltpu.roll(halo_s, (4 - corner) % 8, 0), parts[1])
        parts[1] = jnp.where(sub == 5, pltpu.roll(halo_n, (5 - corner) % 8, 0), parts[1])
        return parts

    westward, eastward = pack(0, 0), pack(6, 7)
    for g in range(2):
        msg_a[pl.ds(8 * g, 8), :] = jnp.where(lon_odd, westward[g], eastward[g])
        msg_b[pl.ds(8 * g, 8), :] = jnp.where(lon_odd, eastward[g], westward[g])


def border_kernel(*refs):
    recv_a, recv_b, edge_hbm = refs[:3]
    outs = refs[8:13]
    edge, rows, sems, out_sems = refs[13:]
    loads = [pltpu.make_async_copy(edge_hbm.at[s], edge.at[s], sems.at[s]) for s in range(2)]
    for copy in loads:
        copy.start()
    lat = lax.axis_index("lat")
    odd = lax.rem(lat, 2) == 1
    total = ROWS * lax.axis_size("lat")
    base = lat * ROWS
    stores = []
    for s in range(2):
        low = s == 0
        e = 0 if low else ROWS - 1
        d = 1 if low else -1
        take_a = odd if low else jnp.logical_not(odd)
        halo = [
            jnp.where(take_a, recv_a[pl.ds(8 * i, 8), :], recv_b[pl.ds(8 * i, 8), :])
            for i in range(PLANES)
        ]
        q_out, m_out, add = halo[:M_AT], halo[M_AT:C_AT], halo[C_AT:]
        loads[s].wait()
        q0, q1, n1, n2 = (
            [edge[s, j * Q_PLANES + i] for i in range(Q_PLANES)] for j in range(4)
        )
        m0, m1, m2 = (
            [edge[s, 4 * Q_PLANES + j * LEVELS + k] for k in range(LEVELS)] for j in range(3)
        )

        def row(q, inward, outward, m, m_in, m_o, at, extra=None, low=low):
            spin = coriolis(base + at, total)
            if low:
                return step_row(q, inward, outward, m, m_in, m_o, spin, extra)
            return step_row(q, outward, inward, m, m_o, m_in, spin, extra)

        n_out = row(q_out, q0, q_out, m_out, m0, None, e - d, add)
        n0 = row(q0, q1, q_out, m0, m1, m_out, e)
        r0 = row(n0, n1, n_out, m0, m1, m_out, e)
        r1 = row(n1, n2, n0, m1, m2, m0, e + d)
        two = pl.ds(6 * s, 2)
        for f in range(FIELDS):
            for k in range(LEVELS):
                i = f * LEVELS + k
                rows[s, f, k, :, e % 8, :] = r0[i]
                rows[s, f, k, :, (e + d) % 8, :] = r1[i]
            stores.append(
                pltpu.make_async_copy(
                    rows.at[s, f, :, :, two, :],
                    outs[f].at[:, 3 * s, :, two, :],
                    out_sems.at[s, f],
                )
            )
            stores[-1].start()
    for copy in stores:
        copy.wait()


SPOTS = (0, 33, 64, 97)


def spots(west_s, west_n, east_s, east_n):
    lane = iota(1)
    out = jnp.zeros((8, 128), jnp.float32)
    for spot, x in zip(SPOTS, (west_s, west_n, east_s, east_n)):
        here = jnp.logical_and(lane >= spot, lane < spot + C_AT)
        out = jnp.where(here, pltpu.roll(x, spot, 1) if spot else x, out)
    return out


def at_spot(lane):
    hit = lane == SPOTS[0]
    for spot in SPOTS[1:]:
        hit = jnp.logical_or(hit, lane == spot)
    return hit


def seam_own_kernel(cols, halos, own):
    lane = iota(1)
    h_s, h_n = halos[0], halos[1]
    w_s, w_n = pltpu.roll(h_s, 2, 0), pltpu.roll(h_n, 2, 0)
    e_s, e_n = pltpu.roll(h_s, 6, 0), pltpu.roll(h_n, 6, 0)
    here = at_spot(lane)
    rim = spots(w_s, w_n, e_s, e_n)
    for f in range(6):
        w, e = pltpu.roll(cols[f], 2, 0), pltpu.roll(cols[f], 6, 0)
        for k in range(LEVELS):
            i = f * LEVELS + k
            x = jnp.where(
                lane < 64,
                pltpu.roll(w, (1 - 32 * k) % 128, 1),
                pltpu.roll(e, (65 - 32 * k) % 128, 1),
            )
            own[i] = jnp.where(here, pltpu.roll(rim, (128 - i) % 128, 1), x)
    back = 128 - C_AT
    rim = spots(*(pltpu.roll(x, back, 1) for x in (w_s, w_n, e_s, e_n)))
    for i in range(Q_PLANES):
        own[C_AT + i] = jnp.where(here, pltpu.roll(rim, (128 - i) % 128, 1), 0.0)


def seam_kernel(*refs):
    recv_a, recv_b, own = refs[:3]
    outs = refs[8:13]
    left, right, sems = refs[13:]
    loads = []
    for f in range(FIELDS):
        loads.append(pltpu.make_async_copy(outs[f].at[:, :, pl.ds(0, 8), :], left.at[f], sems.at[f]))
        loads.append(
            pltpu.make_async_copy(
                outs[f].at[:, :, pl.ds(56, 8), :], right.at[f], sems.at[FIELDS + f]
            )
        )
    for copy in loads:
        copy.start()

    lon_odd = lax.rem(lax.axis_index("lon"), 2) == 1
    lat = lax.axis_index("lat")
    total = ROWS * lax.axis_size("lat")
    sub, lane = iota(0), iota(1)
    pa = [recv_a[pl.ds(8 * g, 8), :] for g in range(2)]
    pb = [recv_b[pl.ds(8 * g, 8), :] for g in range(2)]
    from_west = [jnp.where(lon_odd, a, b) for a, b in zip(pa, pb)]
    from_east = [pltpu.roll(jnp.where(lon_odd, b, a), 64, 1) for a, b in zip(pa, pb)]

    w_s, w_n = pltpu.roll(from_west[1], 5, 0), pltpu.roll(from_west[1], 4, 0)
    turned = pltpu.roll(from_east[1], 64, 1)
    e_s, e_n = pltpu.roll(turned, 2, 0), pltpu.roll(turned, 1, 0)
    corner = spots(w_s, w_n, e_s, e_n)
    at_corner = jnp.logical_and(at_spot(lane), sub == jnp.where(lane < 64, 1, 6))
    row = lax.rem(lane, 64) - 1
    inside = jnp.logical_and(row >= 0, row < ROWS)
    outer = jnp.logical_and(inside, sub // 2 == jnp.where(lane < 64, 0, 3))

    q, m = [], []
    for f in range(6):
        group, j = f // 4, f % 4
        w = pltpu.roll(from_west[group], (8 - 2 * j) % 8, 0)
        e = pltpu.roll(from_east[group], (6 - 2 * j) % 8, 0)
        both = jnp.where(sub < 2, w, e)
        for k in range(LEVELS):
            i = f * LEVELS + k
            x = jnp.where(outer, pltpu.roll(both, (1 - 32 * k) % 128, 1), own[i])
            x = jnp.where(at_corner, pltpu.roll(corner, (128 - i) % 128, 1), x)
            if f < FIELDS:
                q.append(x)
            else:
                m.append(jnp.where(row <= ROWS, x, 0.0))
    brought = [own[C_AT + i] for i in range(Q_PLANES)]
    spin = coriolis(row + lat * ROWS, total)

    def move(x, d, axis):
        return pltpu.roll(x, d % x.shape[axis], axis)

    def shifted(x):
        return move(x, -1, 0), move(x, 1, 0), move(x, -1, 1), move(x, 1, 1)

    masks = [face_masks(m[k], *shifted(m[k])) for k in range(LEVELS)]
    for s in range(2):
        p = pressures(q)
        new_q = [None] * Q_PLANES
        for k in range(LEVELS):
            mine = pick(q, k)
            sides = [shifted(x) for x in mine]
            qe, qw, qn, qs = ([x[i] for x in sides] for i in range(4))
            new = update_level(mine, qe, qw, qn, qs, p[k], *shifted(p[k]), masks[k], spin * m[k])
            for f in range(FIELDS):
                i = f * LEVELS + k
                new_q[i] = new[f] + brought[i] if s == 0 else new[f]
        q = new_q

    for copy in loads:
        copy.wait()
    big_lane = iota(1, (128, 128))
    gap = jnp.zeros((112, 128), jnp.float32)
    for f in range(FIELDS):
        w = e = jnp.zeros((8, 128), jnp.float32)
        for k in range(LEVELS):
            x = q[f * LEVELS + k]
            here = lane // 32 == k
            w = jnp.where(here, pltpu.roll(x, (32 * k - 1) % 128, 1), w)
            e = jnp.where(here, pltpu.roll(x, (32 * k - 65) % 128, 1), e)
        w, e = pltpu.roll(w, 6, 0), pltpu.roll(e, 2, 0)
        turned = jnp.concatenate([w, gap, e], axis=0).T
        a = left[f].reshape(128, 128)
        b = right[f].reshape(128, 128)
        left[f] = jnp.where(big_lane < 2, turned, a).reshape(LEVELS, 4, 8, 128)
        right[f] = jnp.where(big_lane >= 126, turned, b).reshape(LEVELS, 4, 8, 128)
    stores = []
    for f in range(FIELDS):
        stores.append(pltpu.make_async_copy(left.at[f], outs[f].at[:, :, pl.ds(0, 8), :], sems.at[f]))
        stores.append(
            pltpu.make_async_copy(
                right.at[f], outs[f].at[:, :, pl.ds(56, 8), :], sems.at[FIELDS + f]
            )
        )
    for copy in stores:
        copy.start()
    for copy in stores:
        copy.wait()


def view(x):
    return x.reshape(LEVELS, 4, 8, 8, 128).transpose(0, 1, 3, 2, 4)


def unview(x):
    return x.reshape(LEVELS, 4, 8, 8, 128).transpose(0, 1, 3, 2, 4).reshape(LEVELS, ROWS, COLS)


def routes(lons, lats):
    def at(lon, lat):
        return lon * lats + lat

    def other(i, count, shift):
        return ((i + shift) ^ 1) - shift

    lat_a, lat_b, lon_a, lon_b = [], [], [], []
    for lon in range(lons):
        for lat in range(lats):
            me = at(lon, lat)
            lat_a.append((me, at(lon, lat ^ 1)))
            if lat == lats - 1:
                lat_b.append((me, at(lons - 1 - lon, lat)))
            elif lat > 0:
                lat_b.append((me, at(lon, other(lat, lats, 1))))
            lon_a.append((me, at(lon ^ 1, lat)))
            lon_b.append((me, at(other(lon, lons, 1) % lons, lat)))
    return lat_a, lat_b, lon_a, lon_b


def inner_call(args):
    return pl.pallas_call(
        inner_kernel,
        in_specs=[VMEM] * 6,
        out_specs=[HBM] * FIELDS + [VMEM] * 2,
        out_shape=[f32(LEVELS, 4, 64, 128)] * FIELDS
        + [f32(2, EDGE_PLANES, 8, 128), f32(6, 8, 128)],
        scratch_shapes=[
            pltpu.VMEM((4, FIELDS, LEVELS, 64, 128), jnp.float32),
            pltpu.VMEM((8 * (ROWS * Q_PLANES + 2), 128), jnp.float32),
            pltpu.VMEM((8 * (ROWS * Q_PLANES + 2), 128), jnp.float32),
            pltpu.VMEM((8 * (ROWS * LEVELS + 2), 128), jnp.float32),
            pltpu.VMEM((2, 8 * (ROWS * LEVELS + 2), 128), jnp.float32),
            pltpu.VMEM((ROWS, LEVELS, 5, 8, 128), jnp.float32),
            pltpu.SemaphoreType.DMA((4, FIELDS)),
        ],
        compiler_params=params(32),
        cost_estimate=pl.CostEstimate(flops=26 << 20, bytes_accessed=6 << 20, transcendentals=0),
        name="inner_rows",
    )(*args)


def per_device(*args):
    axes = ("lon", "lat")
    lat_a, lat_b, lon_a, lon_b = routes(lax.axis_size("lon"), lax.axis_size("lat"))
    args = [view(x) for x in args]
    out = f32(LEVELS, 4, 64, 128)
    planes = EDGE_PLANES

    split = (LEVELS, 4, 8, 8, 128)
    kept = [jax.ShapeDtypeStruct(split, x.dtype) for x in args]
    send_a, send_b, *args = pl.pallas_call(
        rows_kernel,
        in_specs=[HBM] * 6,
        out_specs=[VMEM] * 8,
        out_shape=[f32(PLANES * 8, 128)] * 2 + kept,
        scratch_shapes=[
            pltpu.VMEM((PLANES * 8, 128), jnp.float32),
            pltpu.SemaphoreType.DMA((4, 6)),
        ],
        compiler_params=params(LIMIT),
        cost_estimate=pl.CostEstimate(flops=1 << 20, bytes_accessed=2 << 20, transcendentals=0),
        name="edge_rows",
    )(*args)
    args = [x.reshape(LEVELS, 4, 64, 128) for x in args]
    recv_b = lax.ppermute(send_b, axes, lat_b)
    recv_a = lax.ppermute(send_a, axes, lat_a)

    *inner, edge, cols = inner_call(args)

    send_la, send_lb, halos = pl.pallas_call(
        columns_kernel,
        in_specs=[VMEM] * 3,
        out_specs=[VMEM] * 3,
        out_shape=[f32(16, 128), f32(16, 128), f32(2, 8, 128)],
        compiler_params=params(16),
        name="edge_columns",
    )(recv_a, recv_b, cols)
    recv_lb = lax.ppermute(send_lb, axes, lon_b)
    recv_la = lax.ppermute(send_la, axes, lon_a)

    border = pl.pallas_call(
        border_kernel,
        in_specs=[VMEM] * 2 + [HBM] * (1 + FIELDS),
        out_specs=[HBM] * FIELDS,
        out_shape=[f32(*split)] * FIELDS,
        input_output_aliases={3 + f: f for f in range(FIELDS)},
        scratch_shapes=[
            pltpu.VMEM((2, planes, 8, 128), jnp.float32),
            pltpu.VMEM((2, FIELDS, LEVELS, 8, 8, 128), jnp.float32),
            pltpu.SemaphoreType.DMA((2,)),
            pltpu.SemaphoreType.DMA((2, FIELDS)),
        ],
        compiler_params=params(24),
        cost_estimate=pl.CostEstimate(flops=4 << 20, bytes_accessed=4 << 20, transcendentals=0),
        name="border_rows",
    )(recv_a, recv_b, edge, *(x.reshape(LEVELS, 4, 8, 8, 128) for x in inner))

    own = pl.pallas_call(
        seam_own_kernel,
        in_specs=[VMEM] * 2,
        out_specs=VMEM,
        out_shape=f32(PLANES, 8, 128),
        compiler_params=params(16),
        cost_estimate=pl.CostEstimate(flops=1 << 20, bytes_accessed=1 << 18, transcendentals=0),
        name="seam_own",
    )(cols, halos)

    final = pl.pallas_call(
        seam_kernel,
        in_specs=[VMEM] * 3 + [HBM] * FIELDS,
        out_specs=[HBM] * FIELDS,
        out_shape=[out] * FIELDS,
        input_output_aliases={3 + f: f for f in range(FIELDS)},
        scratch_shapes=[
            pltpu.VMEM((FIELDS, LEVELS, 4, 8, 128), jnp.float32),
            pltpu.VMEM((FIELDS, LEVELS, 4, 8, 128), jnp.float32),
            pltpu.SemaphoreType.DMA((2 * FIELDS,)),
        ],
        compiler_params=params(16),
        name="seam_columns",
    )(recv_la, recv_lb, own, *(x.reshape(LEVELS, 4, 64, 128) for x in border))
    return tuple(unview(x) for x in final)


def solution(mesh):
    spec = P(None, "lat", "lon")
    return jax.shard_map(
        per_device,
        mesh=mesh,
        in_specs=(spec,) * 6,
        out_specs=(spec,) * 5,
        check_vma=False,
    )
```

```python
import functools

import jax
import jax.numpy as jnp
from jax import lax
from jax.experimental import pallas as pl
from jax.experimental.pallas import tpu as pltpu
from jax.sharding import PartitionSpec as P

ADVECTION = 0.25
DIFFUSION = 0.2
PRESSURE_GAIN = 0.3
EXPAND_T = 0.4
EXPAND_S = 0.6
CORIOLIS_BASE = 0.1
CORIOLIS_SLOPE = 0.4

LEVELS = 4
UNROLL = 8
LIMIT = 53.4
LIMIT_BRING = 50.0
FIELDS = 5
ROWS = 32
COLS = 1024
Q_PLANES = FIELDS * LEVELS
M_AT = Q_PLANES
C_AT = Q_PLANES + LEVELS
PLANES = 2 * Q_PLANES + LEVELS
EDGE_PLANES = 4 * Q_PLANES + 3 * LEVELS
SPEED = ADVECTION * 0.25 / DIFFUSION
SLOPE = PRESSURE_GAIN * 0.5 / DIFFUSION

VMEM = pl.BlockSpec(memory_space=pltpu.VMEM)
HBM = pl.BlockSpec(memory_space=pltpu.HBM)


def params(mib, **more):
    return pltpu.CompilerParams(vmem_limit_bytes=int(mib * (1 << 20)), **more)


def f32(*shape):
    return jax.ShapeDtypeStruct(shape, jnp.float32)


def iota(dim, shape=(8, 128)):
    return lax.broadcasted_iota(jnp.int32, shape, dim)


def east(x):
    near = pltpu.roll(x, 127, 1)
    return jnp.where(iota(1) == 127, pltpu.roll(near, 7, 0), near)


def west(x):
    near = pltpu.roll(x, 1, 1)
    return jnp.where(iota(1) == 0, pltpu.roll(near, 1, 0), near)


def pressures(fields):
    total, out = None, []
    for k in range(LEVELS):
        density = EXPAND_S * fields[3 * LEVELS + k] - EXPAND_T * fields[2 * LEVELS + k]
        half = 0.5 * density
        out.append(half if total is None else total + half)
        total = density if total is None else total + density
    return out


def coriolis(row, total_rows):
    mirrored = jnp.minimum(row, 2 * total_rows - 1 - row)
    return CORIOLIS_BASE + CORIOLIS_SLOPE * (mirrored.astype(jnp.float32) + 0.5) / total_rows


def update_level(q, qe, qw, qn, qs, p, pe, pw, pn, ps, masks, spin):
    me, mw, mn, ms, m0 = masks
    ae = me * (SPEED * (q[0] + qe[0]))
    aw = mw * (SPEED * (q[0] + qw[0]))
    an = mn * (SPEED * (q[1] + qn[1]))
    a_s = ms * (SPEED * (q[1] + qs[1]))
    centre = m0 - ae + aw - an + a_s
    ke, kw, kn, ks = me - ae, mw + aw, mn - an, ms + a_s
    out = [
        centre * q[f] + ke * qe[f] + kw * qw[f] + kn * qn[f] + ks * qs[f] for f in range(FIELDS)
    ]
    gx = SLOPE * (me * (pe - p) + mw * (p - pw))
    gy = SLOPE * (mn * (pn - p) + ms * (p - ps))
    out[0] = out[0] + (spin * q[1] - gx)
    out[1] = out[1] - (spin * q[0] + gy)
    return out


def face_masks(m, m_e, m_w, m_n, m_s):
    scaled = DIFFUSION * m
    me, mw = scaled * m_e, scaled * m_w
    mn = jnp.zeros_like(m) if m_n is None else scaled * m_n
    ms = jnp.zeros_like(m) if m_s is None else scaled * m_s
    return me, mw, mn, ms, m - ((me + mw) + (mn + ms))


def pick(fields, k):
    return [fields[f * LEVELS + k] for f in range(FIELDS)]


def step_row(q, qn, qs, m, mn, ms, spin, add=None):
    p = pressures(q)
    pn, ps = pressures(qn), pressures(qs)
    out = [None] * Q_PLANES
    for k in range(LEVELS):
        own = pick(q, k)
        masks = face_masks(
            m[k],
            east(m[k]),
            west(m[k]),
            None if mn is None else mn[k],
            None if ms is None else ms[k],
        )
        new = update_level(
            own,
            [east(x) for x in own],
            [west(x) for x in own],
            pick(qn, k),
            pick(qs, k),
            p[k],
            east(p[k]),
            west(p[k]),
            pn[k],
            ps[k],
            masks,
            spin * m[k],
        )
        for f in range(FIELDS):
            i = f * LEVELS + k
            out[i] = new[f] if add is None else new[f] + add[i]
    return out


def row_of(ref, k, tile, r):
    return ref[k, tile, pl.ds(r, 8, stride=8), :]


def rows_kernel(*refs):
    args = refs[:6]
    msg_a, msg_b, scratch, floats, ints, sems = refs[6:]
    low, high, copies = [], [], []
    for side, rows in enumerate((low, high)):
        for f in range(6):
            here = floats.at[side, f] if f < FIELDS else ints.at[side]
            rows.append(here)
            two = pl.ds(6 * side, 2)
            tile = args[f].at[:, 3 * side, :, two, :]
            copies.append(pltpu.make_async_copy(tile, here.at[:, :, two, :], sems.at[side, f]))
    for copy in copies:
        copy.start()
    for copy in copies:
        copy.wait()
    lat = lax.axis_index("lat")
    last = lax.axis_size("lat") - 1
    odd = lax.rem(lat, 2) == 1

    def message(tiles, edge, inner, toward):
        q = [tiles[f][k, :, edge, :] for f in range(FIELDS) for k in range(LEVELS)]
        n = [tiles[f][k, :, inner, :] for f in range(FIELDS) for k in range(LEVELS)]
        m = [tiles[5][k, :, edge, :].astype(jnp.float32) for k in range(LEVELS)]
        mi = [tiles[5][k, :, inner, :].astype(jnp.float32) for k in range(LEVELS)]
        p, pi = pressures(q), pressures(n)
        brought = [None] * Q_PLANES
        for k in range(LEVELS):
            mask = DIFFUSION * (m[k] * mi[k])
            a = mask * (SPEED * (q[LEVELS + k] + n[LEVELS + k])) * toward
            ki, ko = mask + a, a - mask
            for f in range(FIELDS):
                i = f * LEVELS + k
                brought[i] = ki * n[i] + ko * q[i]
            i = LEVELS + k
            brought[i] = brought[i] - toward * (SLOPE * mask * (p[k] - pi[k]))
        return q + m + brought

    top = message(high, 7, 6, 1.0)
    bottom = message(low, 0, 1, -1.0)
    for i in range(PLANES):
        msg_a[pl.ds(8 * i, 8), :] = jnp.where(odd, bottom[i], top[i])
        msg_b[pl.ds(8 * i, 8), :] = jnp.where(odd, top[i], bottom[i])

    @pl.when(lat == last)
    def _():
        lane = iota(1)
        for i in range(PLANES):
            x = jnp.take_along_axis(top[i], 127 - lane, axis=1)
            flip = i < 2 * LEVELS or C_AT <= i < C_AT + 2 * LEVELS
            scratch[pl.ds(8 * i, 8), :] = -x if flip else x
        for s in range(8):
            msg_b[pl.ds(7 - s, PLANES, stride=8), :] = scratch[pl.ds(s, PLANES, stride=8), :]


def bring_kernel(*refs):
    args, kept, sems = refs[:6], refs[6:12], refs[12]
    copies = [
        pltpu.make_async_copy(args[f].at[:, t], kept[f].at[:, t], sems.at[f, t])
        for f in range(6)
        for t in range(4)
    ]
    for copy in copies:
        copy.start()
    for copy in copies:
        copy.wait()


def inner_kernel(*refs):
    args, outs = refs[:6], refs[6:11]
    edge, cols = refs[11:13]
    ready, first, second, mask, press, faces, out_sems = refs[13:]
    lat = lax.axis_index("lat")
    total = ROWS * lax.axis_size("lat")
    base = lat * ROWS
    lane = iota(1)

    def at(row, per_row, i, off=0):
        start = pl.multiple_of(8 * (row * per_row + i + 1), 8)
        return pl.ds(start + off, 8)

    def beside(ref, row, per_row, i):
        x = ref[at(row, per_row, i), :]
        after = ref[at(row, per_row, i, 1), :]
        before = ref[at(row, per_row, i, -1), :]
        e = pltpu.roll(jnp.where(lane == 0, after, x), 127, 1)
        w = pltpu.roll(jnp.where(lane == 127, before, x), 1, 1)
        return x, e, w

    def put(tile):
        return [
            pltpu.make_async_copy(ready.at[tile, f], outs[f].at[:, tile], out_sems.at[tile, f])
            for f in range(FIELDS)
        ]

    def step(source, s, r):
        spin = coriolis(base + r, total)
        levels = []
        for k in range(LEVELS):
            sides = [beside(source, r, Q_PLANES, f * LEVELS + k) for f in range(FIELDS)]
            p, pe, pw = beside(press.at[s], r, LEVELS, k)
            if s == 0:
                m, me, mw = beside(mask, r, LEVELS, k)
                mn, ms = mask[at(r + 1, LEVELS, k), :], mask[at(r - 1, LEVELS, k), :]
                face = face_masks(m, me, mw, mn, ms)
                for i in range(5):
                    faces[r, k, i] = face[i]
            else:
                m = mask[at(r, LEVELS, k), :]
                face = [faces[r, k, i] for i in range(5)]
            new = update_level(
                [x[0] for x in sides],
                [x[1] for x in sides],
                [x[2] for x in sides],
                [source[at(r + 1, Q_PLANES, f * LEVELS + k), :] for f in range(FIELDS)],
                [source[at(r - 1, Q_PLANES, f * LEVELS + k), :] for f in range(FIELDS)],
                p,
                pe,
                pw,
                press[s, at(r + 1, LEVELS, k), :],
                press[s, at(r - 1, LEVELS, k), :],
                face,
                spin * m,
            )
            levels.append(new)
        return [levels[k][f] for f in range(FIELDS) for k in range(LEVELS)]

    def step_one(r, c):
        new = step(first, 0, r)
        for i in range(Q_PLANES):
            second[at(r, Q_PLANES, i), :] = new[i]
        for k, p in enumerate(pressures(new)):
            press[1, at(r, LEVELS, k), :] = p
        return c

    def step_two(r, c):
        new = step(second, 1, r)
        tile = r // 8
        for f in range(FIELDS):
            for k in range(LEVELS):
                ready[tile, f, k, pl.ds(r % 8, 8, stride=8), :] = new[f * LEVELS + k]
        return c

    for tile in range(4):
        for r8 in range(8):
            r = tile * 8 + r8
            q = []
            for f in range(FIELDS):
                for k in range(LEVELS):
                    x = row_of(args[f], k, tile, r8)
                    first[at(r, Q_PLANES, f * LEVELS + k), :] = x
                    q.append(x)
            p = pressures(q)
            for k in range(LEVELS):
                m = row_of(args[5], k, tile, r8).astype(jnp.float32)
                mask[at(r, LEVELS, k), :] = m
                press[0, at(r, LEVELS, k), :] = p[k]
        lax.fori_loop(max(1, 8 * tile - 1), 8 * tile + 7, step_one, 0, unroll=UNROLL)
        lax.fori_loop(max(2, 8 * tile - 2), 8 * tile + 6, step_two, 0, unroll=UNROLL)
        if tile > 0:
            for copy in put(tile - 1):
                copy.start()
    for copy in put(3):
        copy.start()

    big_lane = iota(1, (128, 128))
    for f in range(6):
        left = args[f][:, :, pl.ds(0, 8), :].reshape(128, 128).astype(jnp.float32)
        right = args[f][:, :, pl.ds(56, 8), :].reshape(128, 128).astype(jnp.float32)
        both = jnp.where(big_lane < 4, left, pltpu.roll(right, 8, 1))
        cols[f] = both.T[:8]

    for side in range(2):
        e = 0 if side == 0 else ROWS - 1
        d = 1 if side == 0 else -1
        for i in range(Q_PLANES):
            edge[side, i] = first[at(e, Q_PLANES, i), :]
            edge[side, Q_PLANES + i] = first[at(e + d, Q_PLANES, i), :]
            edge[side, 2 * Q_PLANES + i] = second[at(e + d, Q_PLANES, i), :]
            edge[side, 3 * Q_PLANES + i] = second[at(e + 2 * d, Q_PLANES, i), :]
        for k in range(LEVELS):
            for j in range(3):
                edge[side, 4 * Q_PLANES + j * LEVELS + k] = mask[at(e + j * d, LEVELS, k), :]

    for tile in range(4):
        for copy in put(tile):
            copy.wait()


def columns_kernel(recv_a, recv_b, cols, msg_a, msg_b, halos):
    lat_odd = lax.rem(lax.axis_index("lat"), 2) == 1
    lon_odd = lax.rem(lax.axis_index("lon"), 2) == 1
    lane = iota(1, (PLANES, 128))

    def edges(ref):
        left = ref[pl.ds(0, PLANES, stride=8), :]
        right = ref[pl.ds(7, PLANES, stride=8), :]
        return jnp.where(lane < 4, left, pltpu.roll(right, 8, 1))

    from_a, from_b = edges(recv_a), edges(recv_b)
    south = jnp.where(lat_odd, from_a, from_b)
    north = jnp.where(lat_odd, from_b, from_a)
    gap = jnp.zeros((64 - PLANES, 128), jnp.float32)
    turned = jnp.concatenate([south, gap, north, gap], axis=0).T[:8]
    halo_s = turned
    halo_n = pltpu.roll(turned, 64, 1)
    halos[0] = halo_s
    halos[1] = halo_n
    sub = iota(0)

    def pack(at, corner):
        parts = []
        for group in range(2):
            x = jnp.zeros((8, 128), jnp.float32)
            for j in range(4):
                f = group * 4 + j
                if f < 6:
                    y = pltpu.roll(cols[f], (2 * j - at) % 8, 0)
                    x = jnp.where(sub // 2 == j, y, x)
            parts.append(x)
        parts[1] = jnp.where(sub == 4, pltpu.roll(halo_s, (4 - corner) % 8, 0), parts[1])
        parts[1] = jnp.where(sub == 5, pltpu.roll(halo_n, (5 - corner) % 8, 0), parts[1])
        return parts

    westward, eastward = pack(0, 0), pack(6, 7)
    for g in range(2):
        msg_a[pl.ds(8 * g, 8), :] = jnp.where(lon_odd, westward[g], eastward[g])
        msg_b[pl.ds(8 * g, 8), :] = jnp.where(lon_odd, eastward[g], westward[g])


def border_kernel(*refs):
    recv_a, recv_b, edge_hbm = refs[:3]
    outs = refs[8:13]
    edge, rows, sems, out_sems = refs[13:]
    loads = [pltpu.make_async_copy(edge_hbm.at[s], edge.at[s], sems.at[s]) for s in range(2)]
    for copy in loads:
        copy.start()
    lat = lax.axis_index("lat")
    odd = lax.rem(lat, 2) == 1
    total = ROWS * lax.axis_size("lat")
    base = lat * ROWS
    stores = []
    for s in range(2):
        low = s == 0
        e = 0 if low else ROWS - 1
        d = 1 if low else -1
        take_a = odd if low else jnp.logical_not(odd)
        halo = [
            jnp.where(take_a, recv_a[pl.ds(8 * i, 8), :], recv_b[pl.ds(8 * i, 8), :])
            for i in range(PLANES)
        ]
        q_out, m_out, add = halo[:M_AT], halo[M_AT:C_AT], halo[C_AT:]
        loads[s].wait()
        q0, q1, n1, n2 = (
            [edge[s, j * Q_PLANES + i] for i in range(Q_PLANES)] for j in range(4)
        )
        m0, m1, m2 = (
            [edge[s, 4 * Q_PLANES + j * LEVELS + k] for k in range(LEVELS)] for j in range(3)
        )

        def row(q, inward, outward, m, m_in, m_o, at, extra=None, low=low):
            spin = coriolis(base + at, total)
            if low:
                return step_row(q, inward, outward, m, m_in, m_o, spin, extra)
            return step_row(q, outward, inward, m, m_o, m_in, spin, extra)

        n_out = row(q_out, q0, q_out, m_out, m0, None, e - d, add)
        n0 = row(q0, q1, q_out, m0, m1, m_out, e)
        r0 = row(n0, n1, n_out, m0, m1, m_out, e)
        r1 = row(n1, n2, n0, m1, m2, m0, e + d)
        two = pl.ds(6 * s, 2)
        for f in range(FIELDS):
            for k in range(LEVELS):
                i = f * LEVELS + k
                rows[s, f, k, :, e % 8, :] = r0[i]
                rows[s, f, k, :, (e + d) % 8, :] = r1[i]
            stores.append(
                pltpu.make_async_copy(
                    rows.at[s, f, :, :, two, :],
                    outs[f].at[:, 3 * s, :, two, :],
                    out_sems.at[s, f],
                )
            )
            stores[-1].start()
    for copy in stores:
        copy.wait()


SPOTS = (0, 33, 64, 97)


def spots(west_s, west_n, east_s, east_n):
    lane = iota(1)
    out = jnp.zeros((8, 128), jnp.float32)
    for spot, x in zip(SPOTS, (west_s, west_n, east_s, east_n)):
        here = jnp.logical_and(lane >= spot, lane < spot + C_AT)
        out = jnp.where(here, pltpu.roll(x, spot, 1) if spot else x, out)
    return out


def at_spot(lane):
    hit = lane == SPOTS[0]
    for spot in SPOTS[1:]:
        hit = jnp.logical_or(hit, lane == spot)
    return hit


def seam_own_kernel(cols, halos, own):
    lane = iota(1)
    h_s, h_n = halos[0], halos[1]
    w_s, w_n = pltpu.roll(h_s, 2, 0), pltpu.roll(h_n, 2, 0)
    e_s, e_n = pltpu.roll(h_s, 6, 0), pltpu.roll(h_n, 6, 0)
    here = at_spot(lane)
    rim = spots(w_s, w_n, e_s, e_n)
    for f in range(6):
        w, e = pltpu.roll(cols[f], 2, 0), pltpu.roll(cols[f], 6, 0)
        for k in range(LEVELS):
            i = f * LEVELS + k
            x = jnp.where(
                lane < 64,
                pltpu.roll(w, (1 - 32 * k) % 128, 1),
                pltpu.roll(e, (65 - 32 * k) % 128, 1),
            )
            own[i] = jnp.where(here, pltpu.roll(rim, (128 - i) % 128, 1), x)
    back = 128 - C_AT
    rim = spots(*(pltpu.roll(x, back, 1) for x in (w_s, w_n, e_s, e_n)))
    for i in range(Q_PLANES):
        own[C_AT + i] = jnp.where(here, pltpu.roll(rim, (128 - i) % 128, 1), 0.0)


def seam_kernel(*refs):
    recv_b, recv_a, own = refs[:3]
    outs = refs[8:13]
    left, right, turned, sems = refs[13:]
    loads = []
    for f in range(FIELDS):
        loads.append(pltpu.make_async_copy(outs[f].at[:, :, pl.ds(0, 8), :], left.at[f], sems.at[f]))
        loads.append(
            pltpu.make_async_copy(
                outs[f].at[:, :, pl.ds(56, 8), :], right.at[f], sems.at[FIELDS + f]
            )
        )
    for copy in loads:
        copy.start()

    lon_odd = lax.rem(lax.axis_index("lon"), 2) == 1
    lat = lax.axis_index("lat")
    total = ROWS * lax.axis_size("lat")
    sub, lane = iota(0), iota(1)
    pa = [recv_a[pl.ds(8 * g, 8), :] for g in range(2)]
    pb = [recv_b[pl.ds(8 * g, 8), :] for g in range(2)]
    from_west = [jnp.where(lon_odd, a, b) for a, b in zip(pa, pb)]
    from_east = [pltpu.roll(jnp.where(lon_odd, b, a), 64, 1) for a, b in zip(pa, pb)]

    w_s, w_n = pltpu.roll(from_west[1], 5, 0), pltpu.roll(from_west[1], 4, 0)
    back = pltpu.roll(from_east[1], 64, 1)
    e_s, e_n = pltpu.roll(back, 2, 0), pltpu.roll(back, 1, 0)
    corner = spots(w_s, w_n, e_s, e_n)
    at_corner = jnp.logical_and(at_spot(lane), sub == jnp.where(lane < 64, 1, 6))
    row = lax.rem(lane, 64) - 1
    inside = jnp.logical_and(row >= 0, row < ROWS)
    outer = jnp.logical_and(inside, sub // 2 == jnp.where(lane < 64, 0, 3))

    q, m = [], []
    for f in range(6):
        group, j = f // 4, f % 4
        w = pltpu.roll(from_west[group], (8 - 2 * j) % 8, 0)
        e = pltpu.roll(from_east[group], (6 - 2 * j) % 8, 0)
        both = jnp.where(sub < 2, w, e)
        for k in range(LEVELS):
            i = f * LEVELS + k
            x = jnp.where(outer, pltpu.roll(both, (1 - 32 * k) % 128, 1), own[i])
            x = jnp.where(at_corner, pltpu.roll(corner, (128 - i) % 128, 1), x)
            if f < FIELDS:
                q.append(x)
            else:
                m.append(jnp.where(row <= ROWS, x, 0.0))
    brought = [own[C_AT + i] for i in range(Q_PLANES)]
    spin = coriolis(row + lat * ROWS, total)

    def move(x, d, axis):
        return pltpu.roll(x, d % x.shape[axis], axis)

    def shifted(x):
        return move(x, -1, 0), move(x, 1, 0), move(x, -1, 1), move(x, 1, 1)

    masks = [face_masks(m[k], *shifted(m[k])) for k in range(LEVELS)]
    for s in range(2):
        p = pressures(q)
        new_q = [None] * Q_PLANES
        for k in range(LEVELS):
            mine = pick(q, k)
            sides = [shifted(x) for x in mine]
            qe, qw, qn, qs = ([x[i] for x in sides] for i in range(4))
            new = update_level(mine, qe, qw, qn, qs, p[k], *shifted(p[k]), masks[k], spin * m[k])
            for f in range(FIELDS):
                i = f * LEVELS + k
                new_q[i] = new[f] + brought[i] if s == 0 else new[f]
        q = new_q

    big_lane = iota(1, (128, 128))
    gap = jnp.zeros((112, 128), jnp.float32)
    for f in range(FIELDS):
        w = e = jnp.zeros((8, 128), jnp.float32)
        for k in range(LEVELS):
            x = q[f * LEVELS + k]
            here = lane // 32 == k
            w = jnp.where(here, pltpu.roll(x, (32 * k - 1) % 128, 1), w)
            e = jnp.where(here, pltpu.roll(x, (32 * k - 65) % 128, 1), e)
        w, e = pltpu.roll(w, 6, 0), pltpu.roll(e, 2, 0)
        turned[f] = jnp.concatenate([w, gap, e], axis=0).T
    for copy in loads:
        copy.wait()
    for f in range(FIELDS):
        a = left[f].reshape(128, 128)
        b = right[f].reshape(128, 128)
        left[f] = jnp.where(big_lane < 2, turned[f], a).reshape(LEVELS, 4, 8, 128)
        right[f] = jnp.where(big_lane >= 126, turned[f], b).reshape(LEVELS, 4, 8, 128)
    stores = []
    for f in range(FIELDS):
        stores.append(pltpu.make_async_copy(left.at[f], outs[f].at[:, :, pl.ds(0, 8), :], sems.at[f]))
        stores.append(
            pltpu.make_async_copy(
                right.at[f], outs[f].at[:, :, pl.ds(56, 8), :], sems.at[FIELDS + f]
            )
        )
    for copy in stores:
        copy.start()
    for copy in stores:
        copy.wait()


def view(x):
    return x.reshape(LEVELS, 4, 8, 8, 128).transpose(0, 1, 3, 2, 4)


def unview(x):
    return x.reshape(LEVELS, 4, 8, 8, 128).transpose(0, 1, 3, 2, 4).reshape(LEVELS, ROWS, COLS)


def routes(lons, lats):
    def at(lon, lat):
        return lon * lats + lat

    def other(i, count, shift):
        return ((i + shift) ^ 1) - shift

    lat_a, lat_b, lon_a, lon_b = [], [], [], []
    for lon in range(lons):
        for lat in range(lats):
            me = at(lon, lat)
            lat_a.append((me, at(lon, lat ^ 1)))
            if lat == lats - 1:
                lat_b.append((me, at(lons - 1 - lon, lat)))
            elif lat > 0:
                lat_b.append((me, at(lon, other(lat, lats, 1))))
            lon_a.append((me, at(lon ^ 1, lat)))
            lon_b.append((me, at(other(lon, lons, 1) % lons, lat)))
    return lat_a, lat_b, lon_a, lon_b


def inner_call(args):
    return pl.pallas_call(
        inner_kernel,
        in_specs=[VMEM] * 6,
        out_specs=[HBM] * FIELDS + [VMEM] * 2,
        out_shape=[f32(LEVELS, 4, 64, 128)] * FIELDS
        + [f32(2, EDGE_PLANES, 8, 128), f32(6, 8, 128)],
        scratch_shapes=[
            pltpu.VMEM((4, FIELDS, LEVELS, 64, 128), jnp.float32),
            pltpu.VMEM((8 * (ROWS * Q_PLANES + 2), 128), jnp.float32),
            pltpu.VMEM((8 * (ROWS * Q_PLANES + 2), 128), jnp.float32),
            pltpu.VMEM((8 * (ROWS * LEVELS + 2), 128), jnp.float32),
            pltpu.VMEM((2, 8 * (ROWS * LEVELS + 2), 128), jnp.float32),
            pltpu.VMEM((ROWS, LEVELS, 5, 8, 128), jnp.float32),
            pltpu.SemaphoreType.DMA((4, FIELDS)),
        ],
        compiler_params=params(32),
        cost_estimate=pl.CostEstimate(flops=26 << 20, bytes_accessed=6 << 20, transcendentals=0),
        name="inner_rows",
    )(*args)


def per_device(*args):
    axes = ("lon", "lat")
    lat_a, lat_b, lon_a, lon_b = routes(lax.axis_size("lon"), lax.axis_size("lat"))
    args = [view(x) for x in args]
    out = f32(LEVELS, 4, 64, 128)
    planes = EDGE_PLANES

    split = (LEVELS, 4, 8, 8, 128)
    send_a, send_b = pl.pallas_call(
        rows_kernel,
        in_specs=[HBM] * 6,
        out_specs=[VMEM] * 2,
        out_shape=[f32(PLANES * 8, 128)] * 2,
        scratch_shapes=[
            pltpu.VMEM((PLANES * 8, 128), jnp.float32),
            pltpu.VMEM((2, FIELDS, LEVELS, 8, 8, 128), jnp.float32),
            pltpu.VMEM((2, LEVELS, 8, 8, 128), jnp.int32),
            pltpu.SemaphoreType.DMA((2, 6)),
        ],
        compiler_params=params(LIMIT),
        cost_estimate=pl.CostEstimate(flops=1 << 20, bytes_accessed=2 << 20, transcendentals=0),
        name="edge_rows",
    )(*args)
    args = [x.reshape(LEVELS, 4, 64, 128) for x in args]
    recv_b = lax.ppermute(send_b, axes, lat_b)
    recv_a = lax.ppermute(send_a, axes, lat_a)

    args = pl.pallas_call(
        bring_kernel,
        in_specs=[HBM] * 6,
        out_specs=[VMEM] * 6,
        out_shape=[jax.ShapeDtypeStruct(x.shape, x.dtype) for x in args],
        scratch_shapes=[pltpu.SemaphoreType.DMA((6, 4))],
        compiler_params=params(LIMIT_BRING),
        cost_estimate=pl.CostEstimate(flops=0, bytes_accessed=6 << 20, transcendentals=0),
        name="bring_fields",
    )(*args)
    *inner, edge, cols = inner_call(args)

    send_la, send_lb, halos = pl.pallas_call(
        columns_kernel,
        in_specs=[VMEM] * 3,
        out_specs=[VMEM] * 3,
        out_shape=[f32(16, 128), f32(16, 128), f32(2, 8, 128)],
        compiler_params=params(16),
        name="edge_columns",
    )(recv_a, recv_b, cols)
    recv_lb = lax.ppermute(send_lb, axes, lon_b)
    recv_la = lax.ppermute(send_la, axes, lon_a)

    border = pl.pallas_call(
        border_kernel,
        in_specs=[VMEM] * 2 + [HBM] * (1 + FIELDS),
        out_specs=[HBM] * FIELDS,
        out_shape=[f32(*split)] * FIELDS,
        input_output_aliases={3 + f: f for f in range(FIELDS)},
        scratch_shapes=[
            pltpu.VMEM((2, planes, 8, 128), jnp.float32),
            pltpu.VMEM((2, FIELDS, LEVELS, 8, 8, 128), jnp.float32),
            pltpu.SemaphoreType.DMA((2,)),
            pltpu.SemaphoreType.DMA((2, FIELDS)),
        ],
        compiler_params=params(24),
        cost_estimate=pl.CostEstimate(flops=4 << 20, bytes_accessed=4 << 20, transcendentals=0),
        name="border_rows",
    )(recv_a, recv_b, edge, *(x.reshape(LEVELS, 4, 8, 8, 128) for x in inner))

    own = pl.pallas_call(
        seam_own_kernel,
        in_specs=[VMEM] * 2,
        out_specs=VMEM,
        out_shape=f32(PLANES, 8, 128),
        compiler_params=params(16),
        cost_estimate=pl.CostEstimate(flops=1 << 20, bytes_accessed=1 << 18, transcendentals=0),
        name="seam_own",
    )(cols, halos)

    final = pl.pallas_call(
        seam_kernel,
        in_specs=[VMEM] * 3 + [HBM] * FIELDS,
        out_specs=[HBM] * FIELDS,
        out_shape=[out] * FIELDS,
        input_output_aliases={3 + f: f for f in range(FIELDS)},
        scratch_shapes=[
            pltpu.VMEM((FIELDS, LEVELS, 4, 8, 128), jnp.float32),
            pltpu.VMEM((FIELDS, LEVELS, 4, 8, 128), jnp.float32),
            pltpu.VMEM((FIELDS, 128, 128), jnp.float32),
            pltpu.SemaphoreType.DMA((2 * FIELDS,)),
        ],
        compiler_params=params(16),
        name="seam_columns",
    )(recv_lb, recv_la, own, *(x.reshape(LEVELS, 4, 64, 128) for x in border))
    return tuple(unview(x) for x in final)


def solution(mesh):
    spec = P(None, "lat", "lon")
    return jax.shard_map(
        per_device,
        mesh=mesh,
        in_specs=(spec,) * 6,
        out_specs=(spec,) * 5,
        check_vma=False,
    )
```

```python
import functools

import jax
import jax.numpy as jnp
from jax import lax
from jax.experimental import pallas as pl
from jax.experimental.pallas import tpu as pltpu
from jax.sharding import PartitionSpec as P

ADVECTION = 0.25
DIFFUSION = 0.2
PRESSURE_GAIN = 0.3
EXPAND_T = 0.4
EXPAND_S = 0.6
CORIOLIS_BASE = 0.1
CORIOLIS_SLOPE = 0.4

LEVELS = 4
UNROLL = 8
LIMIT = 53.4
LIMIT_BRING = 50.0
FIELDS = 5
ROWS = 32
COLS = 1024
Q_PLANES = FIELDS * LEVELS
M_AT = Q_PLANES
C_AT = Q_PLANES + LEVELS
PLANES = 2 * Q_PLANES + LEVELS
EDGE_PLANES = 4 * Q_PLANES + 3 * LEVELS
SPEED = ADVECTION * 0.25 / DIFFUSION
SLOPE = PRESSURE_GAIN * 0.5 / DIFFUSION

VMEM = pl.BlockSpec(memory_space=pltpu.VMEM)
HBM = pl.BlockSpec(memory_space=pltpu.HBM)


def params(mib, **more):
    return pltpu.CompilerParams(vmem_limit_bytes=int(mib * (1 << 20)), **more)


def f32(*shape):
    return jax.ShapeDtypeStruct(shape, jnp.float32)


def iota(dim, shape=(8, 128)):
    return lax.broadcasted_iota(jnp.int32, shape, dim)


def east(x):
    near = pltpu.roll(x, 127, 1)
    return jnp.where(iota(1) == 127, pltpu.roll(near, 7, 0), near)


def west(x):
    near = pltpu.roll(x, 1, 1)
    return jnp.where(iota(1) == 0, pltpu.roll(near, 1, 0), near)


def pressures(fields):
    total, out = None, []
    for k in range(LEVELS):
        density = EXPAND_S * fields[3 * LEVELS + k] - EXPAND_T * fields[2 * LEVELS + k]
        half = 0.5 * density
        out.append(half if total is None else total + half)
        total = density if total is None else total + density
    return out


def coriolis(row, total_rows):
    mirrored = jnp.minimum(row, 2 * total_rows - 1 - row)
    return CORIOLIS_BASE + CORIOLIS_SLOPE * (mirrored.astype(jnp.float32) + 0.5) / total_rows


def update_level(q, qe, qw, qn, qs, p, pe, pw, pn, ps, masks, spin):
    me, mw, mn, ms, m0 = masks
    ae = me * (SPEED * (q[0] + qe[0]))
    aw = mw * (SPEED * (q[0] + qw[0]))
    an = mn * (SPEED * (q[1] + qn[1]))
    a_s = ms * (SPEED * (q[1] + qs[1]))
    centre = m0 - ae + aw - an + a_s
    ke, kw, kn, ks = me - ae, mw + aw, mn - an, ms + a_s
    out = [
        centre * q[f] + ke * qe[f] + kw * qw[f] + kn * qn[f] + ks * qs[f] for f in range(FIELDS)
    ]
    gx = SLOPE * (me * (pe - p) + mw * (p - pw))
    gy = SLOPE * (mn * (pn - p) + ms * (p - ps))
    out[0] = out[0] + (spin * q[1] - gx)
    out[1] = out[1] - (spin * q[0] + gy)
    return out


def face_masks(m, m_e, m_w, m_n, m_s):
    scaled = DIFFUSION * m
    me, mw = scaled * m_e, scaled * m_w
    mn = jnp.zeros_like(m) if m_n is None else scaled * m_n
    ms = jnp.zeros_like(m) if m_s is None else scaled * m_s
    return me, mw, mn, ms, m - ((me + mw) + (mn + ms))


def pick(fields, k):
    return [fields[f * LEVELS + k] for f in range(FIELDS)]


def step_row(q, qn, qs, m, mn, ms, spin, add=None):
    p = pressures(q)
    pn, ps = pressures(qn), pressures(qs)
    out = [None] * Q_PLANES
    for k in range(LEVELS):
        own = pick(q, k)
        masks = face_masks(
            m[k],
            east(m[k]),
            west(m[k]),
            None if mn is None else mn[k],
            None if ms is None else ms[k],
        )
        new = update_level(
            own,
            [east(x) for x in own],
            [west(x) for x in own],
            pick(qn, k),
            pick(qs, k),
            p[k],
            east(p[k]),
            west(p[k]),
            pn[k],
            ps[k],
            masks,
            spin * m[k],
        )
        for f in range(FIELDS):
            i = f * LEVELS + k
            out[i] = new[f] if add is None else new[f] + add[i]
    return out


def row_of(ref, k, tile, r):
    return ref[k, tile, pl.ds(r, 8, stride=8), :]


def rows_kernel(*refs):
    args = refs[:6]
    msg_a, msg_b, scratch, floats, ints, sems = refs[6:]
    low, high, copies = [], [], []
    for side, rows in enumerate((low, high)):
        for f in range(6):
            here = floats.at[side, f] if f < FIELDS else ints.at[side]
            rows.append(here)
            two = pl.ds(6 * side, 2)
            tile = args[f].at[:, 3 * side, :, two, :]
            copies.append(pltpu.make_async_copy(tile, here.at[:, :, two, :], sems.at[side, f]))
    for copy in copies:
        copy.start()
    for copy in copies:
        copy.wait()
    lat = lax.axis_index("lat")
    last = lax.axis_size("lat") - 1
    odd = lax.rem(lat, 2) == 1

    def message(tiles, edge, inner, toward):
        q = [tiles[f][k, :, edge, :] for f in range(FIELDS) for k in range(LEVELS)]
        n = [tiles[f][k, :, inner, :] for f in range(FIELDS) for k in range(LEVELS)]
        m = [tiles[5][k, :, edge, :].astype(jnp.float32) for k in range(LEVELS)]
        mi = [tiles[5][k, :, inner, :].astype(jnp.float32) for k in range(LEVELS)]
        p, pi = pressures(q), pressures(n)
        brought = [None] * Q_PLANES
        for k in range(LEVELS):
            mask = DIFFUSION * (m[k] * mi[k])
            a = mask * (SPEED * (q[LEVELS + k] + n[LEVELS + k])) * toward
            ki, ko = mask + a, a - mask
            for f in range(FIELDS):
                i = f * LEVELS + k
                brought[i] = ki * n[i] + ko * q[i]
            i = LEVELS + k
            brought[i] = brought[i] - toward * (SLOPE * mask * (p[k] - pi[k]))
        return q + m + brought

    top = message(high, 7, 6, 1.0)
    bottom = message(low, 0, 1, -1.0)
    for i in range(PLANES):
        msg_a[pl.ds(8 * i, 8), :] = jnp.where(odd, bottom[i], top[i])
        msg_b[pl.ds(8 * i, 8), :] = jnp.where(odd, top[i], bottom[i])

    @pl.when(lat == last)
    def _():
        lane = iota(1)
        for i in range(PLANES):
            x = jnp.take_along_axis(top[i], 127 - lane, axis=1)
            flip = i < 2 * LEVELS or C_AT <= i < C_AT + 2 * LEVELS
            scratch[pl.ds(8 * i, 8), :] = -x if flip else x
        for s in range(8):
            msg_b[pl.ds(7 - s, PLANES, stride=8), :] = scratch[pl.ds(s, PLANES, stride=8), :]


def bring_kernel(*refs):
    args, kept, sems = refs[:6], refs[6:12], refs[12]
    copies = [
        pltpu.make_async_copy(args[f], kept[f], sems.at[f, 0]) for f in range(6)
    ]
    for copy in copies:
        copy.start()
    for copy in copies:
        copy.wait()


def inner_kernel(*refs):
    args, outs = refs[:6], refs[6:11]
    edge, cols = refs[11:13]
    ready, first, second, mask, press, faces, out_sems = refs[13:]
    lat = lax.axis_index("lat")
    total = ROWS * lax.axis_size("lat")
    base = lat * ROWS
    lane = iota(1)

    def at(row, per_row, i, off=0):
        start = pl.multiple_of(8 * (row * per_row + i + 1), 8)
        return pl.ds(start + off, 8)

    def beside(ref, row, per_row, i):
        x = ref[at(row, per_row, i), :]
        after = ref[at(row, per_row, i, 1), :]
        before = ref[at(row, per_row, i, -1), :]
        e = pltpu.roll(jnp.where(lane == 0, after, x), 127, 1)
        w = pltpu.roll(jnp.where(lane == 127, before, x), 1, 1)
        return x, e, w

    def put(tile):
        return [
            pltpu.make_async_copy(ready.at[tile, f], outs[f].at[:, tile], out_sems.at[tile, f])
            for f in range(FIELDS)
        ]

    def step(source, s, r):
        spin = coriolis(base + r, total)
        levels = []
        for k in range(LEVELS):
            sides = [beside(source, r, Q_PLANES, f * LEVELS + k) for f in range(FIELDS)]
            p, pe, pw = beside(press.at[s], r, LEVELS, k)
            if s == 0:
                m, me, mw = beside(mask, r, LEVELS, k)
                mn, ms = mask[at(r + 1, LEVELS, k), :], mask[at(r - 1, LEVELS, k), :]
                face = face_masks(m, me, mw, mn, ms)
                for i in range(5):
                    faces[r, k, i] = face[i]
            else:
                m = mask[at(r, LEVELS, k), :]
                face = [faces[r, k, i] for i in range(5)]
            new = update_level(
                [x[0] for x in sides],
                [x[1] for x in sides],
                [x[2] for x in sides],
                [source[at(r + 1, Q_PLANES, f * LEVELS + k), :] for f in range(FIELDS)],
                [source[at(r - 1, Q_PLANES, f * LEVELS + k), :] for f in range(FIELDS)],
                p,
                pe,
                pw,
                press[s, at(r + 1, LEVELS, k), :],
                press[s, at(r - 1, LEVELS, k), :],
                face,
                spin * m,
            )
            levels.append(new)
        return [levels[k][f] for f in range(FIELDS) for k in range(LEVELS)]

    def step_one(r, c):
        new = step(first, 0, r)
        for i in range(Q_PLANES):
            second[at(r, Q_PLANES, i), :] = new[i]
        for k, p in enumerate(pressures(new)):
            press[1, at(r, LEVELS, k), :] = p
        return c

    def step_two(r, c):
        new = step(second, 1, r)
        tile = r // 8
        for f in range(FIELDS):
            for k in range(LEVELS):
                ready[tile, f, k, pl.ds(r % 8, 8, stride=8), :] = new[f * LEVELS + k]
        return c

    for tile in range(4):
        for r8 in range(8):
            r = tile * 8 + r8
            q = []
            for f in range(FIELDS):
                for k in range(LEVELS):
                    x = row_of(args[f], k, tile, r8)
                    first[at(r, Q_PLANES, f * LEVELS + k), :] = x
                    q.append(x)
            p = pressures(q)
            for k in range(LEVELS):
                m = row_of(args[5], k, tile, r8).astype(jnp.float32)
                mask[at(r, LEVELS, k), :] = m
                press[0, at(r, LEVELS, k), :] = p[k]
        lax.fori_loop(max(1, 8 * tile - 1), 8 * tile + 7, step_one, 0, unroll=UNROLL)
        lax.fori_loop(max(2, 8 * tile - 2), 8 * tile + 6, step_two, 0, unroll=UNROLL)
        if tile > 0:
            for copy in put(tile - 1):
                copy.start()
    for copy in put(3):
        copy.start()

    big_lane = iota(1, (128, 128))
    for f in range(6):
        left = args[f][:, :, pl.ds(0, 8), :].reshape(128, 128).astype(jnp.float32)
        right = args[f][:, :, pl.ds(56, 8), :].reshape(128, 128).astype(jnp.float32)
        both = jnp.where(big_lane < 4, left, pltpu.roll(right, 8, 1))
        cols[f] = both.T[:8]

    for side in range(2):
        e = 0 if side == 0 else ROWS - 1
        d = 1 if side == 0 else -1
        for i in range(Q_PLANES):
            edge[side, i] = first[at(e, Q_PLANES, i), :]
            edge[side, Q_PLANES + i] = first[at(e + d, Q_PLANES, i), :]
            edge[side, 2 * Q_PLANES + i] = second[at(e + d, Q_PLANES, i), :]
            edge[side, 3 * Q_PLANES + i] = second[at(e + 2 * d, Q_PLANES, i), :]
        for k in range(LEVELS):
            for j in range(3):
                edge[side, 4 * Q_PLANES + j * LEVELS + k] = mask[at(e + j * d, LEVELS, k), :]

    for tile in range(4):
        for copy in put(tile):
            copy.wait()


def columns_kernel(recv_a, recv_b, cols, msg_a, msg_b, halos):
    lat_odd = lax.rem(lax.axis_index("lat"), 2) == 1
    lon_odd = lax.rem(lax.axis_index("lon"), 2) == 1
    lane = iota(1, (PLANES, 128))

    def edges(ref):
        left = ref[pl.ds(0, PLANES, stride=8), :]
        right = ref[pl.ds(7, PLANES, stride=8), :]
        return jnp.where(lane < 4, left, pltpu.roll(right, 8, 1))

    from_a, from_b = edges(recv_a), edges(recv_b)
    south = jnp.where(lat_odd, from_a, from_b)
    north = jnp.where(lat_odd, from_b, from_a)
    gap = jnp.zeros((64 - PLANES, 128), jnp.float32)
    turned = jnp.concatenate([south, gap, north, gap], axis=0).T[:8]
    halo_s = turned
    halo_n = pltpu.roll(turned, 64, 1)
    halos[0] = halo_s
    halos[1] = halo_n
    sub = iota(0)

    def pack(at, corner):
        parts = []
        for group in range(2):
            x = jnp.zeros((8, 128), jnp.float32)
            for j in range(4):
                f = group * 4 + j
                if f < 6:
                    y = pltpu.roll(cols[f], (2 * j - at) % 8, 0)
                    x = jnp.where(sub // 2 == j, y, x)
            parts.append(x)
        parts[1] = jnp.where(sub == 4, pltpu.roll(halo_s, (4 - corner) % 8, 0), parts[1])
        parts[1] = jnp.where(sub == 5, pltpu.roll(halo_n, (5 - corner) % 8, 0), parts[1])
        return parts

    westward, eastward = pack(0, 0), pack(6, 7)
    for g in range(2):
        msg_a[pl.ds(8 * g, 8), :] = jnp.where(lon_odd, westward[g], eastward[g])
        msg_b[pl.ds(8 * g, 8), :] = jnp.where(lon_odd, eastward[g], westward[g])


def border_kernel(*refs):
    recv_a, recv_b, edge_hbm = refs[:3]
    outs = refs[8:13]
    edge, rows, sems, out_sems = refs[13:]
    loads = [pltpu.make_async_copy(edge_hbm.at[s], edge.at[s], sems.at[s]) for s in range(2)]
    for copy in loads:
        copy.start()
    lat = lax.axis_index("lat")
    odd = lax.rem(lat, 2) == 1
    total = ROWS * lax.axis_size("lat")
    base = lat * ROWS
    stores = []
    for s in range(2):
        low = s == 0
        e = 0 if low else ROWS - 1
        d = 1 if low else -1
        take_a = odd if low else jnp.logical_not(odd)
        halo = [
            jnp.where(take_a, recv_a[pl.ds(8 * i, 8), :], recv_b[pl.ds(8 * i, 8), :])
            for i in range(PLANES)
        ]
        q_out, m_out, add = halo[:M_AT], halo[M_AT:C_AT], halo[C_AT:]
        loads[s].wait()
        q0, q1, n1, n2 = (
            [edge[s, j * Q_PLANES + i] for i in range(Q_PLANES)] for j in range(4)
        )
        m0, m1, m2 = (
            [edge[s, 4 * Q_PLANES + j * LEVELS + k] for k in range(LEVELS)] for j in range(3)
        )

        def row(q, inward, outward, m, m_in, m_o, at, extra=None, low=low):
            spin = coriolis(base + at, total)
            if low:
                return step_row(q, inward, outward, m, m_in, m_o, spin, extra)
            return step_row(q, outward, inward, m, m_o, m_in, spin, extra)

        n_out = row(q_out, q0, q_out, m_out, m0, None, e - d, add)
        n0 = row(q0, q1, q_out, m0, m1, m_out, e)
        r0 = row(n0, n1, n_out, m0, m1, m_out, e)
        r1 = row(n1, n2, n0, m1, m2, m0, e + d)
        two = pl.ds(6 * s, 2)
        for f in range(FIELDS):
            for k in range(LEVELS):
                i = f * LEVELS + k
                rows[s, f, k, :, e % 8, :] = r0[i]
                rows[s, f, k, :, (e + d) % 8, :] = r1[i]
            stores.append(
                pltpu.make_async_copy(
                    rows.at[s, f, :, :, two, :],
                    outs[f].at[:, 3 * s, :, two, :],
                    out_sems.at[s, f],
                )
            )
            stores[-1].start()
    for copy in stores:
        copy.wait()


SPOTS = (0, 33, 64, 97)


def spots(west_s, west_n, east_s, east_n):
    lane = iota(1)
    out = jnp.zeros((8, 128), jnp.float32)
    for spot, x in zip(SPOTS, (west_s, west_n, east_s, east_n)):
        here = jnp.logical_and(lane >= spot, lane < spot + C_AT)
        out = jnp.where(here, pltpu.roll(x, spot, 1) if spot else x, out)
    return out


def at_spot(lane):
    hit = lane == SPOTS[0]
    for spot in SPOTS[1:]:
        hit = jnp.logical_or(hit, lane == spot)
    return hit


def seam_own_kernel(cols, halos, own):
    lane = iota(1)
    h_s, h_n = halos[0], halos[1]
    w_s, w_n = pltpu.roll(h_s, 2, 0), pltpu.roll(h_n, 2, 0)
    e_s, e_n = pltpu.roll(h_s, 6, 0), pltpu.roll(h_n, 6, 0)
    here = at_spot(lane)
    rim = spots(w_s, w_n, e_s, e_n)
    for f in range(6):
        w, e = pltpu.roll(cols[f], 2, 0), pltpu.roll(cols[f], 6, 0)
        for k in range(LEVELS):
            i = f * LEVELS + k
            x = jnp.where(
                lane < 64,
                pltpu.roll(w, (1 - 32 * k) % 128, 1),
                pltpu.roll(e, (65 - 32 * k) % 128, 1),
            )
            own[i] = jnp.where(here, pltpu.roll(rim, (128 - i) % 128, 1), x)
    back = 128 - C_AT
    rim = spots(*(pltpu.roll(x, back, 1) for x in (w_s, w_n, e_s, e_n)))
    for i in range(Q_PLANES):
        own[C_AT + i] = jnp.where(here, pltpu.roll(rim, (128 - i) % 128, 1), 0.0)


def seam_kernel(*refs):
    recv_b, recv_a, own = refs[:3]
    outs = refs[8:13]
    left, right, turned, sems = refs[13:]
    loads = []
    for f in range(FIELDS):
        loads.append(pltpu.make_async_copy(outs[f].at[:, :, pl.ds(0, 8), :], left.at[f], sems.at[f]))
        loads.append(
            pltpu.make_async_copy(
                outs[f].at[:, :, pl.ds(56, 8), :], right.at[f], sems.at[FIELDS + f]
            )
        )
    for copy in loads:
        copy.start()

    lon_odd = lax.rem(lax.axis_index("lon"), 2) == 1
    lat = lax.axis_index("lat")
    total = ROWS * lax.axis_size("lat")
    sub, lane = iota(0), iota(1)
    pa = [recv_a[pl.ds(8 * g, 8), :] for g in range(2)]
    pb = [recv_b[pl.ds(8 * g, 8), :] for g in range(2)]
    from_west = [jnp.where(lon_odd, a, b) for a, b in zip(pa, pb)]
    from_east = [pltpu.roll(jnp.where(lon_odd, b, a), 64, 1) for a, b in zip(pa, pb)]

    w_s, w_n = pltpu.roll(from_west[1], 5, 0), pltpu.roll(from_west[1], 4, 0)
    back = pltpu.roll(from_east[1], 64, 1)
    e_s, e_n = pltpu.roll(back, 2, 0), pltpu.roll(back, 1, 0)
    corner = spots(w_s, w_n, e_s, e_n)
    at_corner = jnp.logical_and(at_spot(lane), sub == jnp.where(lane < 64, 1, 6))
    row = lax.rem(lane, 64) - 1
    inside = jnp.logical_and(row >= 0, row < ROWS)
    outer = jnp.logical_and(inside, sub // 2 == jnp.where(lane < 64, 0, 3))

    q, m = [], []
    for f in range(6):
        group, j = f // 4, f % 4
        w = pltpu.roll(from_west[group], (8 - 2 * j) % 8, 0)
        e = pltpu.roll(from_east[group], (6 - 2 * j) % 8, 0)
        both = jnp.where(sub < 2, w, e)
        for k in range(LEVELS):
            i = f * LEVELS + k
            x = jnp.where(outer, pltpu.roll(both, (1 - 32 * k) % 128, 1), own[i])
            x = jnp.where(at_corner, pltpu.roll(corner, (128 - i) % 128, 1), x)
            if f < FIELDS:
                q.append(x)
            else:
                m.append(jnp.where(row <= ROWS, x, 0.0))
    brought = [own[C_AT + i] for i in range(Q_PLANES)]
    spin = coriolis(row + lat * ROWS, total)

    def move(x, d, axis):
        return pltpu.roll(x, d % x.shape[axis], axis)

    def shifted(x):
        return move(x, -1, 0), move(x, 1, 0), move(x, -1, 1), move(x, 1, 1)

    masks = [face_masks(m[k], *shifted(m[k])) for k in range(LEVELS)]
    for s in range(2):
        p = pressures(q)
        new_q = [None] * Q_PLANES
        for k in range(LEVELS):
            mine = pick(q, k)
            sides = [shifted(x) for x in mine]
            qe, qw, qn, qs = ([x[i] for x in sides] for i in range(4))
            new = update_level(mine, qe, qw, qn, qs, p[k], *shifted(p[k]), masks[k], spin * m[k])
            for f in range(FIELDS):
                i = f * LEVELS + k
                new_q[i] = new[f] + brought[i] if s == 0 else new[f]
        q = new_q

    big_lane = iota(1, (128, 128))
    gap = jnp.zeros((112, 128), jnp.float32)
    for f in range(FIELDS):
        w = e = jnp.zeros((8, 128), jnp.float32)
        for k in range(LEVELS):
            x = q[f * LEVELS + k]
            here = lane // 32 == k
            w = jnp.where(here, pltpu.roll(x, (32 * k - 1) % 128, 1), w)
            e = jnp.where(here, pltpu.roll(x, (32 * k - 65) % 128, 1), e)
        w, e = pltpu.roll(w, 6, 0), pltpu.roll(e, 2, 0)
        turned[f] = jnp.concatenate([w, gap, e], axis=0).T
    for copy in loads:
        copy.wait()
    stores = []
    for f in range(FIELDS):
        a = left[f].reshape(128, 128)
        b = right[f].reshape(128, 128)
        left[f] = jnp.where(big_lane < 2, turned[f], a).reshape(LEVELS, 4, 8, 128)
        right[f] = jnp.where(big_lane >= 126, turned[f], b).reshape(LEVELS, 4, 8, 128)
        stores.append(pltpu.make_async_copy(left.at[f], outs[f].at[:, :, pl.ds(0, 8), :], sems.at[f]))
        stores.append(
            pltpu.make_async_copy(
                right.at[f], outs[f].at[:, :, pl.ds(56, 8), :], sems.at[FIELDS + f]
            )
        )
        stores[-2].start()
        stores[-1].start()
    for copy in stores:
        copy.wait()


def view(x):
    return x.reshape(LEVELS, 4, 8, 8, 128).transpose(0, 1, 3, 2, 4)


def unview(x):
    return x.reshape(LEVELS, 4, 8, 8, 128).transpose(0, 1, 3, 2, 4).reshape(LEVELS, ROWS, COLS)


def routes(lons, lats):
    def at(lon, lat):
        return lon * lats + lat

    def other(i, count, shift):
        return ((i + shift) ^ 1) - shift

    lat_a, lat_b, lon_a, lon_b = [], [], [], []
    for lon in range(lons):
        for lat in range(lats):
            me = at(lon, lat)
            lat_a.append((me, at(lon, lat ^ 1)))
            if lat == lats - 1:
                lat_b.append((me, at(lons - 1 - lon, lat)))
            elif lat > 0:
                lat_b.append((me, at(lon, other(lat, lats, 1))))
            lon_a.append((me, at(lon ^ 1, lat)))
            lon_b.append((me, at(other(lon, lons, 1) % lons, lat)))
    return lat_a, lat_b, lon_a, lon_b


def inner_call(args):
    return pl.pallas_call(
        inner_kernel,
        in_specs=[VMEM] * 6,
        out_specs=[HBM] * FIELDS + [VMEM] * 2,
        out_shape=[f32(LEVELS, 4, 64, 128)] * FIELDS
        + [f32(2, EDGE_PLANES, 8, 128), f32(6, 8, 128)],
        scratch_shapes=[
            pltpu.VMEM((4, FIELDS, LEVELS, 64, 128), jnp.float32),
            pltpu.VMEM((8 * (ROWS * Q_PLANES + 2), 128), jnp.float32),
            pltpu.VMEM((8 * (ROWS * Q_PLANES + 2), 128), jnp.float32),
            pltpu.VMEM((8 * (ROWS * LEVELS + 2), 128), jnp.float32),
            pltpu.VMEM((2, 8 * (ROWS * LEVELS + 2), 128), jnp.float32),
            pltpu.VMEM((ROWS, LEVELS, 5, 8, 128), jnp.float32),
            pltpu.SemaphoreType.DMA((4, FIELDS)),
        ],
        compiler_params=params(32),
        cost_estimate=pl.CostEstimate(flops=26 << 20, bytes_accessed=6 << 20, transcendentals=0),
        name="inner_rows",
    )(*args)


def per_device(*args):
    axes = ("lon", "lat")
    lat_a, lat_b, lon_a, lon_b = routes(lax.axis_size("lon"), lax.axis_size("lat"))
    args = [view(x) for x in args]
    out = f32(LEVELS, 4, 64, 128)
    planes = EDGE_PLANES

    split = (LEVELS, 4, 8, 8, 128)
    send_a, send_b = pl.pallas_call(
        rows_kernel,
        in_specs=[HBM] * 6,
        out_specs=[VMEM] * 2,
        out_shape=[f32(PLANES * 8, 128)] * 2,
        scratch_shapes=[
            pltpu.VMEM((PLANES * 8, 128), jnp.float32),
            pltpu.VMEM((2, FIELDS, LEVELS, 8, 8, 128), jnp.float32),
            pltpu.VMEM((2, LEVELS, 8, 8, 128), jnp.int32),
            pltpu.SemaphoreType.DMA((2, 6)),
        ],
        compiler_params=params(LIMIT),
        cost_estimate=pl.CostEstimate(flops=1 << 20, bytes_accessed=2 << 20, transcendentals=0),
        name="edge_rows",
    )(*args)
    args = [x.reshape(LEVELS, 4, 64, 128) for x in args]
    recv_b = lax.ppermute(send_b, axes, lat_b)
    recv_a = lax.ppermute(send_a, axes, lat_a)

    args = pl.pallas_call(
        bring_kernel,
        in_specs=[HBM] * 6,
        out_specs=[VMEM] * 6,
        out_shape=[jax.ShapeDtypeStruct(x.shape, x.dtype) for x in args],
        scratch_shapes=[pltpu.SemaphoreType.DMA((6, 4))],
        compiler_params=params(LIMIT_BRING),
        cost_estimate=pl.CostEstimate(flops=0, bytes_accessed=6 << 20, transcendentals=0),
        name="bring_fields",
    )(*args)
    *inner, edge, cols = inner_call(args)

    send_la, send_lb, halos = pl.pallas_call(
        columns_kernel,
        in_specs=[VMEM] * 3,
        out_specs=[VMEM] * 3,
        out_shape=[f32(16, 128), f32(16, 128), f32(2, 8, 128)],
        compiler_params=params(16),
        name="edge_columns",
    )(recv_a, recv_b, cols)
    recv_lb = lax.ppermute(send_lb, axes, lon_b)
    recv_la = lax.ppermute(send_la, axes, lon_a)

    border = pl.pallas_call(
        border_kernel,
        in_specs=[VMEM] * 2 + [HBM] * (1 + FIELDS),
        out_specs=[HBM] * FIELDS,
        out_shape=[f32(*split)] * FIELDS,
        input_output_aliases={3 + f: f for f in range(FIELDS)},
        scratch_shapes=[
            pltpu.VMEM((2, planes, 8, 128), jnp.float32),
            pltpu.VMEM((2, FIELDS, LEVELS, 8, 8, 128), jnp.float32),
            pltpu.SemaphoreType.DMA((2,)),
            pltpu.SemaphoreType.DMA((2, FIELDS)),
        ],
        compiler_params=params(24),
        cost_estimate=pl.CostEstimate(flops=4 << 20, bytes_accessed=4 << 20, transcendentals=0),
        name="border_rows",
    )(recv_a, recv_b, edge, *(x.reshape(LEVELS, 4, 8, 8, 128) for x in inner))

    own = pl.pallas_call(
        seam_own_kernel,
        in_specs=[VMEM] * 2,
        out_specs=VMEM,
        out_shape=f32(PLANES, 8, 128),
        compiler_params=params(16),
        cost_estimate=pl.CostEstimate(flops=1 << 20, bytes_accessed=1 << 18, transcendentals=0),
        name="seam_own",
    )(cols, halos)

    final = pl.pallas_call(
        seam_kernel,
        in_specs=[VMEM] * 3 + [HBM] * FIELDS,
        out_specs=[HBM] * FIELDS,
        out_shape=[out] * FIELDS,
        input_output_aliases={3 + f: f for f in range(FIELDS)},
        scratch_shapes=[
            pltpu.VMEM((FIELDS, LEVELS, 4, 8, 128), jnp.float32),
            pltpu.VMEM((FIELDS, LEVELS, 4, 8, 128), jnp.float32),
            pltpu.VMEM((FIELDS, 128, 128), jnp.float32),
            pltpu.SemaphoreType.DMA((2 * FIELDS,)),
        ],
        compiler_params=params(16),
        name="seam_columns",
    )(recv_lb, recv_la, own, *(x.reshape(LEVELS, 4, 64, 128) for x in border))
    return tuple(unview(x) for x in final)


def solution(mesh):
    spec = P(None, "lat", "lon")
    return jax.shard_map(
        per_device,
        mesh=mesh,
        in_specs=(spec,) * 6,
        out_specs=(spec,) * 5,
        check_vma=False,
    )
```
